256 devices in a mesh: gx: 32 (over y, z_hi, x), gy: 8 (over z_lo, core).
Axes of the slice: x: 4, y: 4, z: 8 (z_hi: 2, z_lo: 4; z = z_hi * 4 + z_lo), core: 2. Of those that a mesh axis runs over, the one named last changes fastest.
Arguments:
- forcing: bfloat16 [2, 2, 8, 4096, 640], P(None, None, None, ('gx', 'gy')), may hold values from -100 to 100
- scale: float32 [4096], P(('gx', 'gy')), may hold values from 0.5 to 2
- damping: float32 [4096, 640], P(('gx', 'gy')), may hold values from 0.2 to 2
- volume: float32 [640, 640], replicated, may hold values from -0.25 to 0.25
- lift: float32 [960, 640], replicated, may hold values from -0.1875 to 0.1875
- slots: int32 [32, 32, 4], P('gx', 'gy'), may hold values from 0 to 15, as said below
Outputs:
- response_basis: float32 [2, 2, 8, 4096, 640], P(None, None, None, ('gx', 'gy'))
- triangle_factor: float32 [2, 2, 8, 8], replicated
The draws below stay inside these ranges and needn't reach their ends.
Inputs may be any that keep to these rules, and one draw needn't show every extreme that they name: `slots`: within each device's block of 1 x 4 x 4 elements every storage row 0 to 15 appears once.
All inputs are finite; a program needn't handle non-finite values.
Results may differ from the reference program's by a relative error of at most 0.0003.
Values sent between devices are 32-bit elements; how exact they have to be, the bound alone decides.
A program may use at most 128 MiB of HBM per device.

```python
import math
import jax
import jax.numpy as jnp
from jax import lax

COMPS = 10
NODE_SIDE = 4
NODES = 640
FACE = 160
COLS = 8
STEPS = 2
EXD = 1
EYD = 4
EZD = 4
ELD = 16
EX = 32
EY = 32
ELEMS = 4096
N_GY = 8


def draw_forcing(key, part):
    key = jax.random.fold_in(key, 11)
    devices = ELEMS // ELD
    shape = (2, 2, COLS, ELEMS, NODES)
    along = (jnp.arange(ELEMS) // ELD).astype(jnp.float32) / max(devices - 1, 1)
    col_pos = jnp.arange(COLS).astype(jnp.float32) / max(COLS - 1, 1)
    values = jax.random.truncated_normal(key, -6.0, 6.0, shape, jnp.float32)
    row_gain = 3.0 ** along
    col_gain = 3.0 ** col_pos
    result = values * row_gain[None, None, None, :, None] * col_gain[None, None, :, None, None]
    return result.astype(jnp.bfloat16)


def draw_slots(key, part):
    key = jax.random.fold_in(key, 23)
    along_x = EX // EXD
    along_y = EY // EYD
    scores = jax.random.randint(key, (along_x * along_y, ELD), 0, 1 << 16) * ELD + jnp.arange(ELD, dtype=jnp.int32)
    ranking = jnp.argsort(scores, axis=1).astype(jnp.int32)
    blocks = ranking.reshape(along_x, along_y, EXD, EYD, EZD).transpose(0, 2, 1, 3, 4)
    return blocks.reshape(EX, EY, EZD)


def steps_of(own_key, extent, split, smallest, high):
    def one(position, shards_of):
        steps = jax.random.uniform(jax.random.fold_in(jax.random.fold_in(own_key, 6), position), (shards_of,), jnp.float32, smallest / len(split), high / len(split))
        return jnp.repeat(jnp.exp(steps), extent[position] // shards_of).reshape((-1,) + (1,) * (len(extent) - position - 1))

    factor_of = one(*split[0])
    for cut in split[1:]:
        factor_of = factor_of * one(*cut)
    return factor_of


def normal_values(stream_key, shape, width, bound, kind=jnp.bfloat16):
    return jnp.clip(width * jax.random.normal(stream_key, shape, jnp.float32), -bound, bound).astype(kind)


def setup_inputs(seed: int = 0) -> dict:
    keys = jax.random.split(jax.random.key(seed), 7)
    return {
        "forcing": draw_forcing(jax.random.fold_in(keys[6], 71), 0),
        "scale": jnp.clip(jnp.exp(math.log(2.0) - 1.3862944 * jax.random.uniform(keys[1], (ELEMS,), jnp.float32) ** steps_of(keys[1], (ELEMS,), ((0, 256),), -0.2, 0.2)), 0.5, 2.0),
        "damping": jnp.clip(0.2 + 1.8 * jax.random.uniform(keys[2], (ELEMS, NODES), jnp.float32) ** steps_of(keys[2], (ELEMS, NODES), ((0, 256),), -0.2, 0.2), 0.2, 2.0),
        "volume": normal_values(keys[3], (NODES, NODES), NODES ** -0.5, 0.25, jnp.float32),
        "lift": normal_values(keys[4], (6 * FACE, NODES), (6 * FACE) ** -0.5, 0.1875, jnp.float32),
        "slots": draw_slots(jax.random.fold_in(keys[6], 71), 0),
    }


step_size = 0.4
omegas = (1.3, 3.1)
highest = lax.Precision.HIGHEST

def face_traces(field):
    lead_shape = field.shape[:-1]
    node_cube = field.reshape(lead_shape + (COMPS, NODE_SIDE, NODE_SIDE, NODE_SIDE))
    trace_width = COMPS * NODE_SIDE * NODE_SIDE
    pieces = [node_cube[..., 0, :, :], node_cube[..., NODE_SIDE - 1, :, :], node_cube[..., 0, :], node_cube[..., NODE_SIDE - 1, :], node_cube[..., 0], node_cube[..., NODE_SIDE - 1]]
    return [face_piece.reshape(lead_shape + (trace_width,)) for face_piece in pieces]

def combine(field, scale_grid, damping_grid, volume, lift, jump_terms):
    own_part = scale_grid[..., None] * jnp.dot(field, volume, precision=highest, preferred_element_type=jnp.float32)
    lifted = jnp.dot(jump_terms, lift, precision=highest, preferred_element_type=jnp.float32)
    return own_part - damping_grid * field + lifted

def forcing_at(drive_field, moment):
    result = jnp.zeros_like(drive_field[0, 0])
    for freq_index in range(2):
        angle_now = omegas[freq_index] * moment
        result = result + drive_field[freq_index, 0] * math.cos(angle_now) - drive_field[freq_index, 1] * math.sin(angle_now)
    return result

def march(drive_field, operate):
    state_now = jnp.zeros_like(drive_field[0, 0])
    acc_real = [jnp.zeros_like(state_now), jnp.zeros_like(state_now)]
    acc_imag = [jnp.zeros_like(state_now), jnp.zeros_like(state_now)]
    for step_index in range(STEPS):
        time_now = step_index * step_size
        time_next = time_now + step_size
        slope_one = forcing_at(drive_field, time_now)
        if step_index > 0:
            slope_one = slope_one + operate(state_now)
        trial_state = state_now + step_size * slope_one
        slope_two = operate(trial_state) + forcing_at(drive_field, time_next)
        state_now = state_now + 0.5 * step_size * (slope_one + slope_two)
        for freq_index in range(2):
            angle_next = omegas[freq_index] * time_next
            acc_real[freq_index] = acc_real[freq_index] + step_size * math.cos(angle_next) * state_now
            acc_imag[freq_index] = acc_imag[freq_index] - step_size * math.sin(angle_next) * state_now
    return (jnp.stack(acc_real), jnp.stack(acc_imag))

def spread(value, target):
    return value.reshape((value.shape[0],) + (1,) * (target.ndim - 1))

def cholesky_parts(gram_real, gram_imag):
    columns = gram_real.shape[-1]
    upper_real = {}
    upper_imag = {}
    for row_index in range(columns):
        pivot_square = gram_real[:, row_index, row_index]
        for earlier in range(row_index):
            pivot_square = pivot_square - upper_real[earlier, row_index] ** 2 - upper_imag[earlier, row_index] ** 2
        pivot_value = jnp.sqrt(pivot_square)
        upper_real[row_index, row_index] = pivot_value
        upper_imag[row_index, row_index] = jnp.zeros_like(pivot_value)
        for col_index in range(row_index + 1, columns):
            value_real = gram_real[:, row_index, col_index]
            value_imag = gram_imag[:, row_index, col_index]
            for earlier in range(row_index):
                left_real = upper_real[earlier, row_index]
                left_imag = upper_imag[earlier, row_index]
                right_real = upper_real[earlier, col_index]
                right_imag = upper_imag[earlier, col_index]
                value_real = value_real - (left_real * right_real + left_imag * right_imag)
                value_imag = value_imag - (left_real * right_imag - left_imag * right_real)
            upper_real[row_index, col_index] = value_real / pivot_value
            upper_imag[row_index, col_index] = value_imag / pivot_value
    return (upper_real, upper_imag)

def orthonormalize(acc_real, acc_imag, gram_real, gram_imag, unknowns):
    upper_real, upper_imag = cholesky_parts(gram_real, gram_imag)
    columns = gram_real.shape[-1]
    basis_real = []
    basis_imag = []
    for col_index in range(columns):
        part_real = acc_real[:, col_index]
        part_imag = acc_imag[:, col_index]
        for earlier in range(col_index):
            coef_real = spread(upper_real[earlier, col_index], part_real)
            coef_imag = spread(upper_imag[earlier, col_index], part_real)
            part_real = part_real - (basis_real[earlier] * coef_real - basis_imag[earlier] * coef_imag)
            part_imag = part_imag - (basis_real[earlier] * coef_imag + basis_imag[earlier] * coef_real)
        pivot_value = spread(upper_real[col_index, col_index], part_real)
        basis_real.append(part_real / pivot_value)
        basis_imag.append(part_imag / pivot_value)
    root_total = math.sqrt(unknowns)
    basis_out = jnp.stack([jnp.stack(basis_real, 1), jnp.stack(basis_imag, 1)], 1) * root_total
    zero_entry = jnp.zeros_like(gram_real[:, 0, 0])
    factor_real = jnp.stack([jnp.stack([upper_real.get((row_index, col_index), zero_entry) for col_index in range(columns)], -1) for row_index in range(columns)], -2)
    factor_imag = jnp.stack([jnp.stack([upper_imag.get((row_index, col_index), zero_entry) for col_index in range(columns)], -1) for row_index in range(columns)], -2)
    factor = jnp.stack([factor_real, factor_imag], 1) / root_total
    return (basis_out, factor)

def apply_operator(field, scale_grid, damping_grid, volume, lift):
    own_traces = face_traces(field)
    near_lowx = jnp.pad(own_traces[1], ((1, 0), (0, 0), (0, 0), (0, 0)))[:-1]
    near_highx = jnp.pad(own_traces[0], ((0, 1), (0, 0), (0, 0), (0, 0)))[1:]
    near_lowy = jnp.pad(own_traces[3], ((0, 0), (1, 0), (0, 0), (0, 0)))[:, :-1]
    near_highy = jnp.pad(own_traces[2], ((0, 0), (0, 1), (0, 0), (0, 0)))[:, 1:]
    near_lowz = jnp.roll(own_traces[5], 1, axis=2)
    near_highz = jnp.roll(own_traces[4], -1, axis=2)
    neighbours = [near_lowx, near_highx, near_lowy, near_highy, near_lowz, near_highz]
    jump_terms = jnp.concatenate([neighbours[face_index] - own_traces[face_index] for face_index in range(6)], axis=-1)
    return combine(field, scale_grid, damping_grid, volume, lift, jump_terms)

def reference(forcing, scale, damping, volume, lift, slots):
    index_x = lax.broadcasted_iota(jnp.int32, (EX, EY, EZD), 0)
    index_y = lax.broadcasted_iota(jnp.int32, (EX, EY, EZD), 1)
    owner = index_x // EXD * N_GY + index_y // EYD
    global_rows = (owner * ELD + slots).reshape(-1).astype(jnp.int32)
    scale_grid = scale[global_rows].reshape(EX, EY, EZD)
    damping_grid = damping[global_rows].reshape(EX, EY, EZD, NODES)
    by_column = jnp.moveaxis(forcing, 2, 0)

    def operate(field):
        return apply_operator(field, scale_grid, damping_grid, volume, lift)

    def integrate(column):
        drive_field = column[:, :, global_rows].astype(jnp.float32).reshape(2, 2, EX, EY, EZD, NODES)
        return march(drive_field, operate)
    acc_real, acc_imag = lax.map(integrate, by_column)
    acc_real = jnp.moveaxis(acc_real, 0, 1)
    acc_imag = jnp.moveaxis(acc_imag, 0, 1)
    flat_real = acc_real.reshape(2, COLS, -1)
    flat_imag = acc_imag.reshape(2, COLS, -1)
    gram_real = jnp.einsum('wjn,wkn->wjk', flat_real, flat_real, precision=highest) + jnp.einsum('wjn,wkn->wjk', flat_imag, flat_imag, precision=highest)
    cross_terms = jnp.einsum('wjn,wkn->wjk', flat_real, flat_imag, precision=highest)
    gram_imag = cross_terms - jnp.swapaxes(cross_terms, 1, 2)
    basis_out, factor = orthonormalize(acc_real, acc_imag, gram_real, gram_imag, ELEMS * NODES)
    flat_basis = basis_out.reshape(2, 2, COLS, ELEMS, NODES)
    stored = jnp.zeros((2, 2, COLS, ELEMS, NODES), jnp.float32).at[:, :, :, global_rows].set(flat_basis)
    return (stored, factor)
```

```python
import math

import jax
import jax.numpy as jnp
from jax import lax
from jax.experimental import pallas as pl
from jax.experimental.pallas import tpu as pltpu
from jax.sharding import PartitionSpec as P

NODES = 640
FACE = 160
LANES = 128
KDIM = NODES + 6 * FACE
step_size = 0.4
omegas = (1.3, 3.1)
MESH = pl.DeviceIdType.MESH
f32 = jnp.float32
bf16 = jnp.bfloat16
GROUP = 16


def iota(shape, dim):
    return lax.broadcasted_iota(jnp.int32, shape, dim)


def split(value):
    high = value.astype(bf16)
    return high, (value - high.astype(f32)).astype(bf16)


def mm(left, right):
    return lax.dot_general(left, right, (((1,), (0,)), ((), ())), preferred_element_type=f32)


def lane_slots(slots_ref):
    group = iota((1, LANES), 1) >> 3
    result = jnp.zeros((1, LANES), jnp.int32)
    for g in range(16):
        result = jnp.where(group == g, slots_ref[0, g // 4, g % 4], result)
    return result


def placement(slots_ref):
    row = iota((LANES, LANES), 0)
    lane = iota((LANES, LANES), 1)
    return ((row >> 4) == (lane & 7)) & ((row & 15) == lane_slots(slots_ref))


def march_kernel(
    forcing, scale, damping, volume, lift, slots,
    qh_out, ql_out, gram_out,
    fb, vol, lft, lfy, dmp, wh, wl, f1, f2, st, q1, k1, dt, jump, xb, acc,
    sx, sy, rx, ry, zs, zr,
    load_sem, ssx, rsx, ssy, rsy, ssz, rsz,
):
    gx, gy = lax.axis_index("gx"), lax.axis_index("gy")
    last_x, last_y = lax.axis_size("gx") - 1, lax.axis_size("gy") - 1
    h = step_size

    loads = [
        pltpu.make_async_copy(forcing, fb, load_sem.at[0]),
        pltpu.make_async_copy(damping, dmp, load_sem.at[1]),
        pltpu.make_async_copy(volume, vol, load_sem.at[2]),
        pltpu.make_async_copy(lift, lft, load_sem.at[3]),
    ]
    for load in loads:
        load.start()

    sides = [
        (gx > 0, (gx - 1, gy)),
        (gx < last_x, (gx + 1, gy)),
        (gy > 0, (gx, gy - 1)),
        (gy < last_y, (gx, gy + 1)),
    ]
    yy, zh, xx = gx // 8, (gx // 4) % 2, gx % 4
    mine = [zh * 8 + gy, yy * 4 + xx]

    def partner(phase, k):
        p = (mine[phase] + k) % GROUP
        if phase == 0:
            return (yy * 8 + (p // 8) * 4 + xx, p % 8)
        return ((p // 4) * 8 + zh * 4 + p % 4, gy)

    barrier = pltpu.get_barrier_semaphore()
    expected = 2 * (GROUP - 1)
    for there, place in sides:
        expected = expected + there.astype(jnp.int32)

        @pl.when(there)
        def _():
            pl.semaphore_signal(barrier, inc=1, device_id=place, device_id_type=MESH)

    for phase in range(2):
        for k in range(1, GROUP):
            pl.semaphore_signal(
                barrier, inc=1, device_id=partner(phase, k), device_id_type=MESH
            )

    for side in range(4):
        land = rx if side < 2 else ry

        @pl.when(jnp.logical_not(sides[side][0]))
        def _():
            for r in range(3):
                land[r, side % 2] = jnp.zeros(land.shape[2:], f32)

    place = placement(slots).astype(f32)
    one_hot = place.astype(bf16)
    scale_lane = jnp.zeros((1, LANES), f32)
    slot_of = lane_slots(slots)
    for s in range(16):
        scale_lane = jnp.where(slot_of == s, scale[s], scale_lane)

    loads[0].wait()

    def part(w, p):
        rows = fb[w, p].reshape(LANES, NODES)
        return lax.dot_general(rows, one_hot, (((0,), (0,)), ((), ())), preferred_element_type=f32)

    f00, f01, f10, f11 = part(0, 0), part(0, 1), part(1, 0), part(1, 1)

    def forcing_at(moment):
        a, b = omegas[0] * moment, omegas[1] * moment
        return (
            f00 * math.cos(a) - f01 * math.sin(a) + f10 * math.cos(b) - f11 * math.sin(b)
        )

    k1[...] = f00 + f10
    st[...] = h * k1[...]
    f1[...] = forcing_at(h)
    f2[...] = forcing_at(2 * h)

    lane = iota((1, LANES), 1)
    quarter = lane >> 5
    span = (lane >> 3) & 3

    def copy_to(r, side):
        out, land = (sx, rx) if side < 2 else (sy, ry)
        s_sem, r_sem = (ssx, rsx) if side < 2 else (ssy, rsy)
        return pltpu.make_async_remote_copy(
            src_ref=out.at[r, side % 2],
            dst_ref=land.at[r, 1 - side % 2],
            send_sem=s_sem.at[r, side % 2],
            recv_sem=r_sem.at[r, 1 - side % 2],
            device_id=sides[side][1],
            device_id_type=MESH,
        )

    def arrival(r, side):
        out, land = (sx, rx) if side < 2 else (sy, ry)
        s_sem, r_sem = (ssx, rsx) if side < 2 else (ssy, rsy)
        return pltpu.make_async_remote_copy(
            src_ref=out.at[r, side % 2],
            dst_ref=land.at[r, side % 2],
            send_sem=s_sem.at[r, side % 2],
            recv_sem=r_sem.at[r, side % 2],
            device_id=sides[side][1],
            device_id_type=MESH,
        )

    def y_block(e, high):
        return st[pl.ds((12 if high else 0) + e, 40, stride=16), :]

    def send_faces(r):
        cube = st[...].reshape(10, 64, LANES)
        sx[r, 0] = cube[:, :16].reshape(FACE, LANES)
        sx[r, 1] = cube[:, 48:].reshape(FACE, LANES)
        for side in range(2):
            @pl.when(sides[side][0])
            def _():
                copy_to(r, side).start()
        for high in range(2):
            packed = jnp.zeros((40, LANES), f32)
            for e in range(4):
                shift = (32 * e - (96 if high else 0)) % LANES
                block = y_block(e, high)
                if shift:
                    block = pltpu.roll(block, shift, 1)
                packed = jnp.where(quarter == e, block, packed)
            sy[r, high] = packed

            @pl.when(sides[2 + high][0])
            def _():
                copy_to(r, 2 + high).start()

    def to_operand(row, value):
        high, low = split(value)
        rows = pl.ds(row, value.shape[0])
        xb[rows, 0:LANES] = high
        xb[rows, LANES:] = low

    def products(ranges, first):
        for block in range(5):
            rows = slice(block * 128, block * 128 + 128)
            both = None
            for lo, hi in ranges:
                wide = mm(wh[rows, lo:hi], xb[lo:hi, :])
                term = wide[:, :LANES] + wide[:, LANES:] + mm(wl[rows, lo:hi], xb[lo:hi, :LANES])
                both = term if both is None else both + term
            acc[rows, :] = both if first else acc[rows, :] + both

    def operate(r):
        state = st[...]
        to_operand(0, scale_lane * state)
        low = st[pl.ds(0, FACE, stride=4), :]
        high = st[pl.ds(3, FACE, stride=4), :]
        near = jnp.where(span == 0, pltpu.roll(high, LANES - 24, 1), pltpu.roll(high, 8, 1))
        to_operand(NODES + 4 * FACE, near - low)
        near = jnp.where(span == 3, pltpu.roll(low, 24, 1), pltpu.roll(low, LANES - 8, 1))
        to_operand(NODES + 5 * FACE, near - high)
        products([(0, NODES), (NODES + 4 * FACE, KDIM)], True)
        for side in (2, 3):
            @pl.when(sides[side][0])
            def _():
                arrival(r, side).wait_recv()
        for e in range(4):
            rows = slice(40 * e, 40 * e + 40)
            low, high = y_block(e, 0), y_block(e, 1)
            far = ry[r, 0]
            if e:
                far = pltpu.roll(far, LANES - 32 * e, 1)
            jump[rows, :] = jnp.where(quarter == 0, far, pltpu.roll(high, 32, 1)) - low
            far = ry[r, 1]
            if e < 3:
                far = pltpu.roll(far, 96 - 32 * e, 1)
            rows = slice(FACE + 40 * e, FACE + 40 * e + 40)
            jump[rows, :] = jnp.where(quarter == 3, far, pltpu.roll(low, LANES - 32, 1)) - high
        to_operand(NODES + 2 * FACE, jump[...])
        for side in (0, 1):
            @pl.when(sides[side][0])
            def _():
                arrival(r, side).wait_recv()
            to_operand(NODES + side * FACE, rx[r, side] - sx[r, side])
        products([(NODES, NODES + 4 * FACE)], False)
        acc[...] = acc[...] - dt[...] * state

    pl.semaphore_wait(barrier, expected)
    send_faces(0)

    loads[1].wait()
    spread16 = jnp.where(iota((16, LANES), 0) == slot_of, 1.0, 0.0).astype(bf16)
    rest = dmp[...]
    total = jnp.zeros((NODES, LANES), f32)
    for _ in range(3):
        piece = rest.astype(bf16)
        rest = rest - piece.astype(f32)
        total = total + lax.dot_general(
            piece, spread16, (((0,), (0,)), ((), ())), preferred_element_type=f32
        )
    dt[...] = total

    def turn(source, column):
        high, low = split(source.T)
        wh[:, column : column + source.shape[0]] = high
        wl[:, column : column + source.shape[0]] = low

    loads[2].wait()
    for block in range(5):
        turn(vol[block * 128 : block * 128 + 128, :], block * 128)
    loads[3].wait()
    for b in range(5):
        columns = slice(b * 128, b * 128 + 128)
        lfy[b] = lft[2 * FACE : 4 * FACE, columns]
        for high in range(2):
            for e in range(4):
                row = 2 * FACE + high * FACE + 40 * e
                lft[row : row + 40, columns] = lfy[b, pl.ds(high * FACE + e, 40, stride=4), :]
    for block in range(7):
        turn(lft[block * 128 : block * 128 + 128, :], NODES + block * 128)
    turn(lft[896:960, :], NODES + 896)

    operate(0)
    k2 = acc[...] + f1[...]
    q1[...] = 0.5 * h * (k1[...] + k2)
    st[...] = q1[...]
    send_faces(1)
    operate(1)
    k1[...] = acc[...] + f1[...]
    st[...] = q1[...] + h * k1[...]
    send_faces(2)
    operate(2)
    k2 = acc[...] + f2[...]
    first = q1[...]
    second = first + 0.5 * h * (k1[...] + k2)

    qh, ql = split(jnp.concatenate([first, second], axis=1))
    th, tl = split(jnp.concatenate([first.T, second.T], axis=0))
    qh_out[...] = th
    ql_out[...] = tl
    pairs = mm(th, qh) + (mm(th, ql) + mm(tl, qh)) + mm(tl, ql)
    row = iota((2 * LANES, 2 * LANES), 0)
    col = iota((2 * LANES, 2 * LANES), 1)
    pairs = jnp.where(((row >> 3) & 15) == ((col >> 3) & 15), pairs, 0.0)
    sums = jnp.sum(pairs.reshape(2, 16, 8, 2 * LANES), axis=1)
    halves = []
    for half in range(2):
        value = sums[:, :, half * LANES : half * LANES + LANES].reshape(16, LANES)
        for shift in (64, 32, 16, 8):
            value = value + pltpu.roll(value, shift, 1)
        halves.append(value)
    both = jnp.where((lane & 8) == 0, halves[0], halves[1])
    sub = iota((8, LANES), 0)
    wide = iota((8, LANES), 1)
    for t in range(2):
        picked = jnp.where((wide >> 4) == sub, both[8 * t : 8 * t + 8], 0.0)
        zs[0, t : t + 1, :] = jnp.sum(picked, axis=0, keepdims=True)

    for phase in range(2):
        copies = []
        for k in range(1, GROUP):
            copy = pltpu.make_async_remote_copy(
                src_ref=zs.at[phase],
                dst_ref=zr.at[phase, mine[phase]],
                send_sem=ssz.at[phase, k],
                recv_sem=rsz.at[phase, mine[phase]],
                device_id=partner(phase, k),
                device_id_type=MESH,
            )
            copy.start()
            copies.append(copy)
        zr[phase, mine[phase]] = zs[phase]
        for k in range(1, GROUP):
            source = (mine[phase] + k) % GROUP
            pltpu.make_async_remote_copy(
                src_ref=zs.at[phase],
                dst_ref=zr.at[phase, source],
                send_sem=ssz.at[phase, k],
                recv_sem=rsz.at[phase, source],
                device_id=partner(phase, k),
                device_id_type=MESH,
            ).wait_recv()
        total = zr[phase, 0]
        for s in range(1, GROUP):
            total = total + zr[phase, s]
        if phase == 0:
            zs[1] = total
        else:
            gram_out[...] = total
        for copy in copies:
            copy.wait_send()

    for r in range(3):
        for side in range(4):
            @pl.when(sides[side][0])
            def _():
                copy_to(r, side).wait_send()


def finish_kernel(unknowns, qh, ql, gram, slots, basis_out, factor_out, stage, sems):
    sub = iota((8, LANES), 0)
    lane = iota((8, LANES), 1)
    tiles = []
    for t in range(2):
        value = jnp.where((lane >> 4) == sub, gram[t : t + 1, :], 0.0)
        for shift in (64, 32, 16):
            value = value + pltpu.roll(value, shift, 1)
        tiles.append(value)
    low = (lane & 8) == 0
    a11 = jnp.where(low, tiles[0], pltpu.roll(tiles[0], 8, 1))
    a12 = jnp.where(low, pltpu.roll(tiles[0], LANES - 8, 1), tiles[0])
    a21 = jnp.where(low, tiles[1], pltpu.roll(tiles[1], 8, 1))
    a22 = jnp.where(low, pltpu.roll(tiles[1], LANES - 8, 1), tiles[1])
    root = math.sqrt(unknowns)
    keep = (iota((LANES, LANES), 0) & 15) == lane_slots(slots)
    h = step_size
    work = []
    for w in range(2):
        angle = omegas[w] * h
        work.append([
            a11 + a22 + math.cos(angle) * (a12 + a21),
            math.sin(angle) * (a21 - a12),
            jnp.where((lane & 7) == sub, 1.0, 0.0),
            jnp.zeros((8, LANES), f32),
        ])
    for i in range(8):
        below, here = sub > i, sub == i
        for w in range(2):
            g_re, g_im, m_re, m_im = work[w]
            c_re = jnp.sum(jnp.where(lane == i, g_re, 0.0), axis=1, keepdims=True)
            c_im = jnp.sum(jnp.where(lane == i, g_im, 0.0), axis=1, keepdims=True)
            pivot = c_re[i : i + 1, :]
            inverse = 1.0 / jnp.sqrt(pivot)
            c_re = c_re / pivot
            c_im = c_im / pivot

            def update(re, im):
                r_re, r_im = re[i : i + 1, :], im[i : i + 1, :]
                new_re = re - (c_re * r_re - c_im * r_im)
                new_im = im - (c_re * r_im + c_im * r_re)
                return (
                    jnp.where(below, new_re, jnp.where(here, re * inverse, re)),
                    jnp.where(below, new_im, jnp.where(here, im * inverse, im)),
                )

            g_re, g_im = update(g_re, g_im)
            m_re, m_im = update(m_re, m_im)
            work[w] = [g_re, g_im, m_re, m_im]
    copies = []
    q_high, q_low = qh[...], ql[...]
    for w in range(2):
        g_re, g_im, m_re, m_im = work[w]
        factor_out[w, 0] = jnp.where(lane >= sub, g_re * (h / root), 0.0)[:, :8]
        factor_out[w, 1] = jnp.where(lane > sub, g_im * (h / root), 0.0)[:, :8]
        for p in range(2):
            blocks = []
            for n in range(2):
                c, s = math.cos(omegas[w] * h * (n + 1)), math.sin(omegas[w] * h * (n + 1))
                if p == 0:
                    coef = root * (c * m_re - s * m_im)
                else:
                    coef = -root * (s * m_re + c * m_im)
                coef = jnp.broadcast_to(coef[:, None, :], (8, 16, LANES)).reshape(LANES, LANES)
                blocks.append(jnp.where(keep, coef, 0.0))
            high, low_part = split(jnp.concatenate(blocks, axis=1))
            result = mm(high, q_high) + (mm(high, q_low) + mm(low_part, q_high))
            stage[w, p] = result.reshape(8, 16, NODES)
            copy = pltpu.make_async_copy(stage.at[w, p], basis_out.at[w, p], sems.at[w, p])
            copy.start()
            copies.append(copy)
    for copy in copies:
        copy.wait()


def on_device(forcing, scale, damping, volume, lift, slots):
    any_space = pl.BlockSpec(memory_space=pl.ANY)
    smem = pl.BlockSpec(memory_space=pltpu.SMEM)
    vmem = pl.BlockSpec(memory_space=pltpu.VMEM)
    state = pltpu.VMEM((NODES, LANES), f32)
    q_high, q_low, gram = pl.pallas_call(
        march_kernel,
        out_shape=(
            jax.ShapeDtypeStruct((2 * LANES, NODES), bf16),
            jax.ShapeDtypeStruct((2 * LANES, NODES), bf16),
            jax.ShapeDtypeStruct((2, LANES), f32),
        ),
        in_specs=[any_space, smem, any_space, any_space, any_space, smem],
        out_specs=(vmem, vmem, vmem),
        scratch_shapes=[
            pltpu.VMEM(forcing.shape, bf16),
            pltpu.VMEM((NODES, NODES), f32),
            pltpu.VMEM((6 * FACE, NODES), f32),
            pltpu.VMEM((5, 2 * FACE, LANES), f32),
            pltpu.VMEM((16, NODES), f32),
            pltpu.VMEM((NODES, KDIM), bf16),
            pltpu.VMEM((NODES, KDIM), bf16),
            state, state, state, state, state, state,
            pltpu.VMEM((2 * FACE, LANES), f32),
            pltpu.VMEM((KDIM, 2 * LANES), bf16),
            state,
            pltpu.VMEM((3, 2, FACE, LANES), f32),
            pltpu.VMEM((3, 2, 40, LANES), f32),
            pltpu.VMEM((3, 2, FACE, LANES), f32),
            pltpu.VMEM((3, 2, 40, LANES), f32),
            pltpu.VMEM((2, 2, LANES), f32),
            pltpu.VMEM((2, GROUP, 2, LANES), f32),
            pltpu.SemaphoreType.DMA((4,)),
            pltpu.SemaphoreType.DMA((3, 2)),
            pltpu.SemaphoreType.DMA((3, 2)),
            pltpu.SemaphoreType.DMA((3, 2)),
            pltpu.SemaphoreType.DMA((3, 2)),
            pltpu.SemaphoreType.DMA((2, GROUP)),
            pltpu.SemaphoreType.DMA((2, GROUP)),
        ],
        compiler_params=pltpu.CompilerParams(
            collective_id=0, has_side_effects=True, vmem_limit_bytes=48 * 1024 * 1024
        ),
        name="march",
    )(forcing, scale, damping, volume, lift, slots)
    unknowns = forcing.shape[3] * NODES * lax.axis_size("gx") * lax.axis_size("gy")
    shape = forcing.shape
    return pl.pallas_call(
        lambda *refs: finish_kernel(unknowns, *refs),
        out_shape=(
            jax.ShapeDtypeStruct(shape, f32),
            jax.ShapeDtypeStruct((2, 2, 8, 8), f32),
        ),
        in_specs=[vmem, vmem, vmem, smem],
        out_specs=(any_space, vmem),
        scratch_shapes=[pltpu.VMEM(shape, f32), pltpu.SemaphoreType.DMA((2, 2))],
        compiler_params=pltpu.CompilerParams(vmem_limit_bytes=32 * 1024 * 1024),
        name="finish",
    )(q_high, q_low, gram, slots)


def solution(mesh):
    placed = (
        P(None, None, None, ("gx", "gy"), None),
        P(("gx", "gy")),
        P(("gx", "gy"), None),
        P(),
        P(),
        P("gx", "gy", None),
    )
    return jax.shard_map(
        on_device,
        mesh=mesh,
        in_specs=placed,
        out_specs=(P(None, None, None, ("gx", "gy"), None), P()),
        check_vma=False,
    )
```

```python
import math

import jax
import jax.numpy as jnp
from jax import lax
from jax.experimental import pallas as pl
from jax.experimental.pallas import tpu as pltpu
from jax.sharding import PartitionSpec as P

NODES = 640
FACE = 160
LANES = 128
KDIM = NODES + 6 * FACE
step_size = 0.4
omegas = (1.3, 3.1)
MESH = pl.DeviceIdType.MESH
f32 = jnp.float32
bf16 = jnp.bfloat16
GROUP = 16


def iota(shape, dim):
    return lax.broadcasted_iota(jnp.int32, shape, dim)


def split(value):
    high = value.astype(bf16)
    return high, (value - high.astype(f32)).astype(bf16)


def mm(left, right):
    return lax.dot_general(left, right, (((1,), (0,)), ((), ())), preferred_element_type=f32)


def lane_slots(slots_ref):
    group = iota((1, LANES), 1) >> 3
    result = jnp.zeros((1, LANES), jnp.int32)
    for g in range(16):
        result = jnp.where(group == g, slots_ref[0, g // 4, g % 4], result)
    return result


def placement(slots_ref):
    row = iota((LANES, LANES), 0)
    lane = iota((LANES, LANES), 1)
    return ((row >> 4) == (lane & 7)) & ((row & 15) == lane_slots(slots_ref))


def march_kernel(
    forcing, scale_hbm, damping, volume, lift, slots_hbm,
    qh_out, ql_out, gram_out,
    slots, scale, fb, vol, lft, lfy, dmp, wh, wl, f1, f2, st, q1, k1, dt, jump, xb, acc,
    qh, ql, th, tl, corr,
    sx, sy, rx, ry, zs, zr,
    load_sem, ssx, rsx, ssy, rsy, ssz, rsz, out_sem,
):
    gx, gy = lax.axis_index("gx"), lax.axis_index("gy")
    last_x, last_y = lax.axis_size("gx") - 1, lax.axis_size("gy") - 1
    h = step_size

    pairs = [
        (slots_hbm, slots),
        (forcing.at[0, 0], fb.at[0, 0]),
        (forcing.at[1, 0], fb.at[1, 0]),
        (scale_hbm, scale),
        (volume, vol),
        (lift, lft),
        (damping, dmp),
        (forcing.at[0, 1], fb.at[0, 1]),
        (forcing.at[1, 1], fb.at[1, 1]),
    ]
    loads = [
        pltpu.make_async_copy(source, target, load_sem.at[n])
        for n, (source, target) in enumerate(pairs)
    ]

    sides = [
        (gx > 0, (gx - 1, gy)),
        (gx < last_x, (gx + 1, gy)),
        (gy > 0, (gx, gy - 1)),
        (gy < last_y, (gx, gy + 1)),
    ]
    yy, zh, xx = gx // 8, (gx // 4) % 2, gx % 4
    mine = [zh * 8 + gy, yy * 4 + xx]

    def partner(phase, k):
        p = (mine[phase] + k) % GROUP
        if phase == 0:
            return (yy * 8 + (p // 8) * 4 + xx, p % 8)
        return ((p // 4) * 8 + zh * 4 + p % 4, gy)

    far_side = [
        jnp.logical_and(gx > 0, xx == 0),
        jnp.logical_and(gx < last_x, xx == 3),
    ]

    barrier = pltpu.get_barrier_semaphore()
    expected = 2 * (GROUP - 1)
    for there, place in sides:
        expected = expected + there.astype(jnp.int32)

        @pl.when(there)
        def _():
            pl.semaphore_signal(barrier, inc=1, device_id=place, device_id_type=MESH)

    for load in loads:
        load.start()
    for phase in range(2):
        for k in range(1, GROUP):
            pl.semaphore_signal(
                barrier, inc=1, device_id=partner(phase, k), device_id_type=MESH
            )

    for side in range(4):
        land = rx if side < 2 else ry

        @pl.when(jnp.logical_not(sides[side][0]))
        def _():
            for r in range(3):
                land[r, side % 2] = jnp.zeros(land.shape[2:], f32)

    loads[0].wait()
    one_hot = placement(slots).astype(f32).astype(bf16)
    slot_of = lane_slots(slots)

    def part(w, p):
        rows = fb[w, p].reshape(LANES, NODES)
        return lax.dot_general(rows, one_hot, (((0,), (0,)), ((), ())), preferred_element_type=f32)

    loads[1].wait()
    loads[2].wait()
    f00, f10 = part(0, 0), part(1, 0)
    k1[...] = f00 + f10
    st[...] = h * k1[...]

    lane = iota((1, LANES), 1)
    quarter = lane >> 5
    span = (lane >> 3) & 3

    def copy_to(r, side):
        out, land = (sx, rx) if side < 2 else (sy, ry)
        s_sem, r_sem = (ssx, rsx) if side < 2 else (ssy, rsy)
        return pltpu.make_async_remote_copy(
            src_ref=out.at[r, side % 2],
            dst_ref=land.at[r, 1 - side % 2],
            send_sem=s_sem.at[r, side % 2],
            recv_sem=r_sem.at[r, 1 - side % 2],
            device_id=sides[side][1],
            device_id_type=MESH,
        )

    def arrival(r, side):
        out, land = (sx, rx) if side < 2 else (sy, ry)
        s_sem, r_sem = (ssx, rsx) if side < 2 else (ssy, rsy)
        return pltpu.make_async_remote_copy(
            src_ref=out.at[r, side % 2],
            dst_ref=land.at[r, side % 2],
            send_sem=s_sem.at[r, side % 2],
            recv_sem=r_sem.at[r, side % 2],
            device_id=sides[side][1],
            device_id_type=MESH,
        )

    def y_block(e, high):
        return st[pl.ds((12 if high else 0) + e, 40, stride=16), :]

    def face(side):
        start = 48 if side else 0
        return st[...].reshape(10, 64, LANES)[:, start : start + 16].reshape(FACE, LANES)

    def send_x(r, side, when):
        @pl.when(when)
        def _():
            sx[r, side] = face(side)
            copy_to(r, side).start()

    def send_y(r):
        for high in range(2):
            packed = jnp.zeros((40, LANES), f32)
            for e in range(4):
                shift = (32 * e - (96 if high else 0)) % LANES
                block = y_block(e, high)
                if shift:
                    block = pltpu.roll(block, shift, 1)
                packed = jnp.where(quarter == e, block, packed)

            @pl.when(sides[2 + high][0])
            def _():
                sy[r, high] = packed
                copy_to(r, 2 + high).start()

    def to_operand(row, value):
        high, low = split(value)
        rows = pl.ds(row, value.shape[0])
        xb[rows, 0:LANES] = high
        xb[rows, LANES:] = low

    def products(ranges, done):
        for block in range(5):
            rows = slice(block * 128, block * 128 + 128)
            both = None
            for lo, hi in ranges:
                wide = mm(wh[rows, lo:hi], xb[lo:hi, :])
                term = wide[:, :LANES] + wide[:, LANES:] + mm(wl[rows, lo:hi], xb[lo:hi, :LANES])
                both = term if both is None else both + term
            done(rows, both)

    def begin(rows, value):
        acc[rows, :] = value

    def add(rows, value):
        acc[rows, :] = acc[rows, :] + value

    def far_value(rows, value):
        st[rows, :] = st[rows, :] + 0.5 * h * value

    X_ROWS = [(NODES, NODES + 2 * FACE)]

    def operate(r):
        state = st[...]
        to_operand(0, scale_lane * state)
        low = st[pl.ds(0, FACE, stride=4), :]
        high = st[pl.ds(3, FACE, stride=4), :]
        near = jnp.where(span == 0, pltpu.roll(high, LANES - 24, 1), pltpu.roll(high, 8, 1))
        to_operand(NODES + 4 * FACE, near - low)
        near = jnp.where(span == 3, pltpu.roll(low, 24, 1), pltpu.roll(low, LANES - 8, 1))
        to_operand(NODES + 5 * FACE, near - high)
        products([(0, NODES), (NODES + 4 * FACE, KDIM)], begin)
        for side in (2, 3):
            @pl.when(sides[side][0])
            def _():
                arrival(r, side).wait_recv()
        for e in range(4):
            rows = slice(40 * e, 40 * e + 40)
            low, high = y_block(e, 0), y_block(e, 1)
            far = ry[r, 0]
            if e:
                far = pltpu.roll(far, LANES - 32 * e, 1)
            jump[rows, :] = jnp.where(quarter == 0, far, pltpu.roll(high, 32, 1)) - low
            far = ry[r, 1]
            if e < 3:
                far = pltpu.roll(far, 96 - 32 * e, 1)
            rows = slice(FACE + 40 * e, FACE + 40 * e + 40)
            jump[rows, :] = jnp.where(quarter == 3, far, pltpu.roll(low, LANES - 32, 1)) - high
        to_operand(NODES + 2 * FACE, jump[...])
        for side in (0, 1):
            near_side = jnp.logical_and(sides[side][0], jnp.logical_not(far_side[side]))

            @pl.when(near_side if r == 0 else sides[side][0])
            def _():
                arrival(r, side).wait_recv()

            if r == 2:
                to_operand(NODES + side * FACE, rx[r, side] - face(side))
            else:
                @pl.when(jnp.logical_not(far_side[side]))
                def _():
                    to_operand(NODES + side * FACE, rx[r, side] - face(side))

                @pl.when(far_side[side])
                def _():
                    value = -face(side) if r == 0 else rx[r, side] + corr[...] - face(side)
                    to_operand(NODES + side * FACE, value)
        products([(NODES, NODES + 4 * FACE)], add)
        acc[...] = acc[...] - dt[...] * state

    pl.semaphore_wait(barrier, expected)
    for side in range(2):
        send_x(0, side, sides[side][0])
    send_y(0)

    loads[3].wait()
    scale_lane = jnp.zeros((1, LANES), f32)
    for s in range(16):
        scale_lane = jnp.where(slot_of == s, scale[s], scale_lane)
    def turn(source, column):
        high, low = split(source.T)
        wh[:, column : column + source.shape[0]] = high
        wl[:, column : column + source.shape[0]] = low

    loads[4].wait()
    for block in range(5):
        turn(vol[block * 128 : block * 128 + 128, :], block * 128)
    loads[5].wait()
    for b in range(5):
        columns = slice(b * 128, b * 128 + 128)
        lfy[b] = lft[2 * FACE : 4 * FACE, columns]
        for high in range(2):
            for e in range(4):
                row = 2 * FACE + high * FACE + 40 * e
                lft[row : row + 40, columns] = lfy[b, pl.ds(high * FACE + e, 40, stride=4), :]
    for block in range(7):
        turn(lft[block * 128 : block * 128 + 128, :], NODES + block * 128)
    turn(lft[896:960, :], NODES + 896)

    loads[6].wait()
    spread16 = jnp.where(iota((16, LANES), 0) == slot_of, 1.0, 0.0).astype(bf16)
    rest = dmp[...]
    total = jnp.zeros((NODES, LANES), f32)
    for _ in range(3):
        piece = rest.astype(bf16)
        rest = rest - piece.astype(f32)
        total = total + lax.dot_general(
            piece, spread16, (((0,), (0,)), ((), ())), preferred_element_type=f32
        )
    dt[...] = total

    loads[7].wait()
    loads[8].wait()
    f00, f01, f10, f11 = part(0, 0), part(0, 1), part(1, 0), part(1, 1)

    def forcing_at(moment):
        a, b = omegas[0] * moment, omegas[1] * moment
        return (
            f00 * math.cos(a) - f01 * math.sin(a) + f10 * math.cos(b) - f11 * math.sin(b)
        )

    f1[...] = forcing_at(h)
    f2[...] = forcing_at(2 * h)

    operate(0)
    st[...] = 0.5 * h * (k1[...] + acc[...] + f1[...])
    for side in range(2):
        send_x(1, side, far_side[side])

        @pl.when(far_side[side])
        def _():
            other = 1 - side
            start = 48 if other else 0
            to_operand(NODES + side * FACE, jnp.zeros((FACE, LANES), f32))
            to_operand(NODES + other * FACE, sx[0, side])
            lo, hi = X_ROWS[0]
            rows = [slice(64 * f + start, 64 * f + start + 16) for f in range(10)]
            left_high = jnp.concatenate([wh[r, lo:hi] for r in rows], axis=0)
            left_low = jnp.concatenate([wl[r, lo:hi] for r in rows], axis=0)
            wide = mm(left_high, xb[lo:hi, :])
            value = wide[:, :LANES] + wide[:, LANES:] + mm(left_low, xb[lo:hi, :LANES])
            corr[...] = 0.5 * h * value
            to_operand(NODES + other * FACE, jnp.zeros((FACE, LANES), f32))
            arrival(0, side).wait_recv()
            to_operand(NODES + side * FACE, rx[0, side])
            products(X_ROWS, far_value)

    for side in range(2):
        send_x(1, side, jnp.logical_and(sides[side][0], jnp.logical_not(far_side[side])))
    send_y(1)
    q1[...] = st[...]

    def keep_state(n, value):
        lanes = slice(n * LANES, n * LANES + LANES)
        high, low = split(value)
        qh[:, lanes] = high
        ql[:, lanes] = low
        high, low = split(value.T)
        th[lanes, :] = high
        tl[lanes, :] = low

    operate(1)
    k1[...] = acc[...] + f1[...]
    st[...] = q1[...] + h * k1[...]
    for side in range(2):
        send_x(2, side, sides[side][0])
    send_y(2)
    keep_state(0, q1[...])
    operate(2)
    keep_state(1, q1[...] + 0.5 * h * (k1[...] + acc[...] + f2[...]))
    results = [
        pltpu.make_async_copy(th, qh_out, out_sem.at[0]),
        pltpu.make_async_copy(tl, ql_out, out_sem.at[1]),
    ]
    for result in results:
        result.start()

    pairs = mm(th[...], qh[...]) + (mm(th[...], ql[...]) + mm(tl[...], qh[...])) + mm(tl[...], ql[...])
    row = iota((2 * LANES, 2 * LANES), 0)
    col = iota((2 * LANES, 2 * LANES), 1)
    pairs = jnp.where(((row >> 3) & 15) == ((col >> 3) & 15), pairs, 0.0)
    sums = jnp.sum(pairs.reshape(2, 16, 8, 2 * LANES), axis=1)
    halves = []
    for half in range(2):
        value = sums[:, :, half * LANES : half * LANES + LANES].reshape(16, LANES)
        for shift in (64, 32, 16, 8):
            value = value + pltpu.roll(value, shift, 1)
        halves.append(value)
    both = jnp.where((lane & 8) == 0, halves[0], halves[1])
    sub = iota((8, LANES), 0)
    wide = iota((8, LANES), 1)
    for t in range(2):
        picked = jnp.where((wide >> 4) == sub, both[8 * t : 8 * t + 8], 0.0)
        zs[0, t : t + 1, :] = jnp.sum(picked, axis=0, keepdims=True)

    for phase in range(2):
        copies = []
        for k in range(1, GROUP):
            copy = pltpu.make_async_remote_copy(
                src_ref=zs.at[phase],
                dst_ref=zr.at[phase, mine[phase]],
                send_sem=ssz.at[phase, k],
                recv_sem=rsz.at[phase, mine[phase]],
                device_id=partner(phase, k),
                device_id_type=MESH,
            )
            copy.start()
            copies.append(copy)
        zr[phase, mine[phase]] = zs[phase]
        for k in range(1, GROUP):
            source = (mine[phase] + k) % GROUP
            pltpu.make_async_remote_copy(
                src_ref=zs.at[phase],
                dst_ref=zr.at[phase, source],
                send_sem=ssz.at[phase, k],
                recv_sem=rsz.at[phase, source],
                device_id=partner(phase, k),
                device_id_type=MESH,
            ).wait_recv()
        total = zr[phase, 0]
        for s in range(1, GROUP):
            total = total + zr[phase, s]
        if phase == 0:
            zs[1] = total
        else:
            gram_out[...] = total
        for copy in copies:
            copy.wait_send()

    for r in range(3):
        for side in range(4):
            @pl.when(sides[side][0])
            def _():
                copy_to(r, side).wait_send()

    for result in results:
        result.wait()


def finish_kernel(
    unknowns, qh_hbm, ql_hbm, gram, slots_hbm, basis_out, factor_out,
    slots, qh, ql, stage, factor, load_sem, sems, factor_sem,
):
    loads = [
        pltpu.make_async_copy(slots_hbm, slots, load_sem.at[0]),
        pltpu.make_async_copy(qh_hbm, qh, load_sem.at[1]),
        pltpu.make_async_copy(ql_hbm, ql, load_sem.at[2]),
    ]
    for load in loads:
        load.start()
    sub = iota((8, LANES), 0)
    lane = iota((8, LANES), 1)
    tiles = []
    for t in range(2):
        value = jnp.where((lane >> 4) == sub, gram[t : t + 1, :], 0.0)
        for shift in (64, 32, 16):
            value = value + pltpu.roll(value, shift, 1)
        tiles.append(value)
    low = (lane & 8) == 0
    a11 = jnp.where(low, tiles[0], pltpu.roll(tiles[0], 8, 1))
    a12 = jnp.where(low, pltpu.roll(tiles[0], LANES - 8, 1), tiles[0])
    a21 = jnp.where(low, tiles[1], pltpu.roll(tiles[1], 8, 1))
    a22 = jnp.where(low, pltpu.roll(tiles[1], LANES - 8, 1), tiles[1])
    root = math.sqrt(unknowns)
    h = step_size
    work = []
    for w in range(2):
        angle = omegas[w] * h
        work.append([
            a11 + a22 + math.cos(angle) * (a12 + a21),
            math.sin(angle) * (a21 - a12),
            jnp.where((lane & 7) == sub, 1.0, 0.0),
            jnp.zeros((8, LANES), f32),
        ])
    for i in range(8):
        below, here = sub > i, sub == i
        for w in range(2):
            g_re, g_im, m_re, m_im = work[w]
            c_re = jnp.sum(jnp.where(lane == i, g_re, 0.0), axis=1, keepdims=True)
            c_im = jnp.sum(jnp.where(lane == i, g_im, 0.0), axis=1, keepdims=True)
            pivot = c_re[i : i + 1, :]
            inverse = 1.0 / jnp.sqrt(pivot)
            c_re = c_re / pivot
            c_im = c_im / pivot

            def update(re, im):
                r_re, r_im = re[i : i + 1, :], im[i : i + 1, :]
                new_re = re - (c_re * r_re - c_im * r_im)
                new_im = im - (c_re * r_im + c_im * r_re)
                return (
                    jnp.where(below, new_re, jnp.where(here, re * inverse, re)),
                    jnp.where(below, new_im, jnp.where(here, im * inverse, im)),
                )

            g_re, g_im = update(g_re, g_im)
            m_re, m_im = update(m_re, m_im)
            work[w] = [g_re, g_im, m_re, m_im]
    for w in range(2):
        g_re, g_im = work[w][:2]
        factor[w, 0] = jnp.where(lane >= sub, g_re * (h / root), 0.0)[:, :8]
        factor[w, 1] = jnp.where(lane > sub, g_im * (h / root), 0.0)[:, :8]
    copies = [pltpu.make_async_copy(factor, factor_out, factor_sem)]
    copies[0].start()
    for load in loads:
        load.wait()
    keep = (iota((LANES, LANES), 0) & 15) == lane_slots(slots)
    q_high, q_low = qh[...], ql[...]
    for w in range(2):
        m_re, m_im = work[w][2:]
        for p in range(2):
            blocks = []
            for n in range(2):
                c, s = math.cos(omegas[w] * h * (n + 1)), math.sin(omegas[w] * h * (n + 1))
                if p == 0:
                    coef = root * (c * m_re - s * m_im)
                else:
                    coef = -root * (s * m_re + c * m_im)
                coef = jnp.broadcast_to(coef[:, None, :], (8, 16, LANES)).reshape(LANES, LANES)
                blocks.append(jnp.where(keep, coef, 0.0))
            high, low_part = split(jnp.concatenate(blocks, axis=1))
            result = mm(high, q_high) + (mm(high, q_low) + mm(low_part, q_high))
            stage[w, p] = result.reshape(8, 16, NODES)
            copy = pltpu.make_async_copy(stage.at[w, p], basis_out.at[w, p], sems.at[w, p])
            copy.start()
            copies.append(copy)
    for copy in copies:
        copy.wait()


def on_device(forcing, scale, damping, volume, lift, slots):
    hbm = pl.BlockSpec(memory_space=pltpu.HBM)
    vmem = pl.BlockSpec(memory_space=pltpu.VMEM)
    state = pltpu.VMEM((NODES, LANES), f32)
    q_high, q_low, gram = pl.pallas_call(
        march_kernel,
        out_shape=(
            jax.ShapeDtypeStruct((2 * LANES, NODES), bf16),
            jax.ShapeDtypeStruct((2 * LANES, NODES), bf16),
            jax.ShapeDtypeStruct((2, LANES), f32),
        ),
        in_specs=[hbm] * 6,
        out_specs=(hbm, hbm, vmem),
        scratch_shapes=[
            pltpu.SMEM(slots.shape, jnp.int32),
            pltpu.SMEM(scale.shape, f32),
            pltpu.VMEM(forcing.shape, bf16),
            pltpu.VMEM((NODES, NODES), f32),
            pltpu.VMEM((6 * FACE, NODES), f32),
            pltpu.VMEM((5, 2 * FACE, LANES), f32),
            pltpu.VMEM((16, NODES), f32),
            pltpu.VMEM((NODES, KDIM), bf16),
            pltpu.VMEM((NODES, KDIM), bf16),
            state, state, state, state, state, state,
            pltpu.VMEM((2 * FACE, LANES), f32),
            pltpu.VMEM((KDIM, 2 * LANES), bf16),
            state,
            pltpu.VMEM((NODES, 2 * LANES), bf16),
            pltpu.VMEM((NODES, 2 * LANES), bf16),
            pltpu.VMEM((2 * LANES, NODES), bf16),
            pltpu.VMEM((2 * LANES, NODES), bf16),
            pltpu.VMEM((FACE, LANES), f32),
            pltpu.VMEM((3, 2, FACE, LANES), f32),
            pltpu.VMEM((3, 2, 40, LANES), f32),
            pltpu.VMEM((3, 2, FACE, LANES), f32),
            pltpu.VMEM((3, 2, 40, LANES), f32),
            pltpu.VMEM((2, 2, LANES), f32),
            pltpu.VMEM((2, GROUP, 2, LANES), f32),
            pltpu.SemaphoreType.DMA((9,)),
            pltpu.SemaphoreType.DMA((3, 2)),
            pltpu.SemaphoreType.DMA((3, 2)),
            pltpu.SemaphoreType.DMA((3, 2)),
            pltpu.SemaphoreType.DMA((3, 2)),
            pltpu.SemaphoreType.DMA((2, GROUP)),
            pltpu.SemaphoreType.DMA((2, GROUP)),
            pltpu.SemaphoreType.DMA((2,)),
        ],
        compiler_params=pltpu.CompilerParams(
            collective_id=0, has_side_effects=True, vmem_limit_bytes=64 * 1024 * 1024
        ),
        name="march",
    )(forcing, scale, damping, volume, lift, slots)
    unknowns = forcing.shape[3] * NODES * lax.axis_size("gx") * lax.axis_size("gy")
    shape = forcing.shape
    return pl.pallas_call(
        lambda *refs: finish_kernel(unknowns, *refs),
        out_shape=(
            jax.ShapeDtypeStruct(shape, f32),
            jax.ShapeDtypeStruct((2, 2, 8, 8), f32),
        ),
        in_specs=[hbm, hbm, vmem, hbm],
        out_specs=(hbm, hbm),
        scratch_shapes=[
            pltpu.SMEM(slots.shape, jnp.int32),
            pltpu.VMEM((2 * LANES, NODES), bf16),
            pltpu.VMEM((2 * LANES, NODES), bf16),
            pltpu.VMEM(shape, f32),
            pltpu.VMEM((2, 2, 8, 8), f32),
            pltpu.SemaphoreType.DMA((3,)),
            pltpu.SemaphoreType.DMA((2, 2)),
            pltpu.SemaphoreType.DMA,
        ],
        compiler_params=pltpu.CompilerParams(vmem_limit_bytes=64 * 1024 * 1024),
        name="finish",
    )(q_high, q_low, gram, slots)


def solution(mesh):
    placed = (
        P(None, None, None, ("gx", "gy"), None),
        P(("gx", "gy")),
        P(("gx", "gy"), None),
        P(),
        P(),
        P("gx", "gy", None),
    )
    return jax.shard_map(
        on_device,
        mesh=mesh,
        in_specs=placed,
        out_specs=(P(None, None, None, ("gx", "gy"), None), P()),
        check_vma=False,
    )
```

```python
import math

import jax
import jax.numpy as jnp
from jax import lax
from jax.experimental import pallas as pl
from jax.experimental.pallas import tpu as pltpu
from jax.sharding import PartitionSpec as P

NODES = 640
FACE = 160
LANES = 128
KDIM = NODES + 6 * FACE
step_size = 0.4
omegas = (1.3, 3.1)
MESH = pl.DeviceIdType.MESH
f32 = jnp.float32
bf16 = jnp.bfloat16
GROUP = 16


def iota(shape, dim):
    return lax.broadcasted_iota(jnp.int32, shape, dim)


def split(value):
    high = value.astype(bf16)
    return high, (value - high.astype(f32)).astype(bf16)


def mm(left, right):
    return lax.dot_general(left, right, (((1,), (0,)), ((), ())), preferred_element_type=f32)


def lane_slots(slots_ref):
    group = iota((1, LANES), 1) >> 3
    result = jnp.zeros((1, LANES), jnp.int32)
    for g in range(16):
        result = jnp.where(group == g, slots_ref[0, g // 4, g % 4], result)
    return result


def placement(slots_ref):
    row = iota((LANES, LANES), 0)
    lane = iota((LANES, LANES), 1)
    return ((row >> 4) == (lane & 7)) & ((row & 15) == lane_slots(slots_ref))


def march_kernel(
    forcing, scale_hbm, damping, volume, lift, slots_hbm,
    qh_out, ql_out, gram_out,
    slots, scale, fb, vol, lft, lfy, dmp, wh, wl, f1, f2, st, q1, k1, dt, jump, xb, acc,
    qh, ql, th, tl, corr, gst, sd, rd,
    sx, sy, rx, ry, zs, zr,
    load_sem, ssx, rsx, ssy, rsy, ssd, rsd, ssz, rsz, out_sem,
):
    gx, gy = lax.axis_index("gx"), lax.axis_index("gy")
    last_x, last_y = lax.axis_size("gx") - 1, lax.axis_size("gy") - 1
    h = step_size

    pairs = [
        (slots_hbm, slots),
        (forcing.at[0, 0], fb.at[0, 0]),
        (forcing.at[1, 0], fb.at[1, 0]),
        (scale_hbm, scale),
        (volume, vol),
        (lift, lft),
        (damping, dmp),
        (forcing.at[0, 1], fb.at[0, 1]),
        (forcing.at[1, 1], fb.at[1, 1]),
    ]
    loads = [
        pltpu.make_async_copy(source, target, load_sem.at[n])
        for n, (source, target) in enumerate(pairs)
    ]

    sides = [
        (gx > 0, (gx - 1, gy)),
        (gx < last_x, (gx + 1, gy)),
        (gy > 0, (gx, gy - 1)),
        (gy < last_y, (gx, gy + 1)),
    ]
    yy, zh, xx = gx // 8, (gx // 4) % 2, gx % 4
    mine = [zh * 8 + gy, yy * 4 + xx]

    def partner(phase, k):
        p = (mine[phase] + k) % GROUP
        if phase == 0:
            return (yy * 8 + (p // 8) * 4 + xx, p % 8)
        return ((p // 4) * 8 + zh * 4 + p % 4, gy)

    far_side = [
        jnp.logical_and(gx > 0, xx == 0),
        jnp.logical_and(gx < last_x, xx == 3),
    ]

    far_any = jnp.logical_or(far_side[0], far_side[1])
    near_side = [
        jnp.logical_and(sides[n][0], jnp.logical_not(far_side[n])) for n in range(2)
    ]
    far_y = [jnp.logical_and(sides[2 + n][0], far_any) for n in range(2)]
    all_x, all_y = [sides[0][0], sides[1][0]], [sides[2][0], sides[3][0]]
    x_sends = [all_x, far_side, near_side, far_side, near_side]
    y_sends = [all_y, far_y, all_y, [], all_y, far_y]

    barrier = pltpu.get_barrier_semaphore()
    expected = 2 * (GROUP - 1)
    for there, place in sides:
        expected = expected + there.astype(jnp.int32)

        @pl.when(there)
        def _():
            pl.semaphore_signal(barrier, inc=1, device_id=place, device_id_type=MESH)

    for load in loads:
        load.start()
    for phase in range(2):
        for k in range(1, GROUP):
            pl.semaphore_signal(
                barrier, inc=1, device_id=partner(phase, k), device_id_type=MESH
            )

    for side in range(4):
        land = rx if side < 2 else ry

        @pl.when(jnp.logical_not(sides[side][0]))
        def _():
            for r in range(land.shape[0]):
                land[r, side % 2] = jnp.zeros(land.shape[2:], f32)

    loads[0].wait()
    one_hot = placement(slots).astype(f32).astype(bf16)
    slot_of = lane_slots(slots)

    def part(w, p):
        rows = fb[w, p].reshape(LANES, NODES)
        return lax.dot_general(rows, one_hot, (((0,), (0,)), ((), ())), preferred_element_type=f32)

    loads[1].wait()
    loads[2].wait()
    f00, f10 = part(0, 0), part(1, 0)
    k1[...] = f00 + f10
    st[...] = h * k1[...]

    lane = iota((1, LANES), 1)
    quarter = lane >> 5
    span = (lane >> 3) & 3

    def copy_to(r, side):
        out, land = (sx, rx) if side < 2 else (sy, ry)
        s_sem, r_sem = (ssx, rsx) if side < 2 else (ssy, rsy)
        return pltpu.make_async_remote_copy(
            src_ref=out.at[r, side % 2],
            dst_ref=land.at[r, 1 - side % 2],
            send_sem=s_sem.at[r, side % 2],
            recv_sem=r_sem.at[r, 1 - side % 2],
            device_id=sides[side][1],
            device_id_type=MESH,
        )

    def arrival(r, side):
        out, land = (sx, rx) if side < 2 else (sy, ry)
        s_sem, r_sem = (ssx, rsx) if side < 2 else (ssy, rsy)
        return pltpu.make_async_remote_copy(
            src_ref=out.at[r, side % 2],
            dst_ref=land.at[r, side % 2],
            send_sem=s_sem.at[r, side % 2],
            recv_sem=r_sem.at[r, side % 2],
            device_id=sides[side][1],
            device_id_type=MESH,
        )

    def y_block(src, e, high):
        return src[pl.ds((12 if high else 0) + e, 40, stride=16), :]

    def face(src, side):
        start = 48 if side else 0
        return src[...].reshape(10, 64, LANES)[:, start : start + 16].reshape(FACE, LANES)

    def send_x(r, side, src, when=None):
        @pl.when(x_sends[r][side] if when is None else when)
        def _():
            sx[r, side] = face(src, side)
            copy_to(r, side).start()

    def send_y(r, src):
        for high in range(2):
            packed = jnp.zeros((40, LANES), f32)
            for e in range(4):
                shift = (32 * e - (96 if high else 0)) % LANES
                block = y_block(src, e, high)
                if shift:
                    block = pltpu.roll(block, shift, 1)
                packed = jnp.where(quarter == e, block, packed)

            @pl.when(y_sends[r][high])
            def _():
                sy[r, high] = packed
                copy_to(r, 2 + high).start()

    def to_operand(row, value):
        high, low = split(value)
        rows = pl.ds(row, value.shape[0])
        xb[rows, 0:LANES] = high
        xb[rows, LANES:] = low

    def products(ranges, done):
        for block in range(5):
            rows = slice(block * 128, block * 128 + 128)
            both = None
            for lo, hi in ranges:
                wide = mm(wh[rows, lo:hi], xb[lo:hi, :])
                term = wide[:, :LANES] + wide[:, LANES:] + mm(wl[rows, lo:hi], xb[lo:hi, :LANES])
                both = term if both is None else both + term
            done(rows, both)

    def begin(rows, value):
        acc[rows, :] = value

    def add(rows, value):
        acc[rows, :] = acc[rows, :] + value

    def far_value(rows, value):
        st[rows, :] = st[rows, :] + 0.5 * h * value

    def ghost_value(rows, value):
        gst[rows, :] = 0.5 * h * value

    X_ROWS = [(NODES, NODES + 2 * FACE)]
    FACE_ROWS = [(NODES, NODES + 4 * FACE)]

    def face_products(side, ranges):
        start = 48 if side else 0
        rows = [slice(64 * f + start, 64 * f + start + 16) for f in range(10)]
        total = None
        for lo, hi in ranges:
            left_high = jnp.concatenate([wh[r, lo:hi] for r in rows], axis=0)
            left_low = jnp.concatenate([wl[r, lo:hi] for r in rows], axis=0)
            wide = mm(left_high, xb[lo:hi, :])
            value = wide[:, :LANES] + wide[:, LANES:] + mm(left_low, xb[lo:hi, :LANES])
            total = value if total is None else total + value
        return total

    def set_x(side, value):
        to_operand(NODES + side * FACE, value)

    def span_jumps(src):
        low = src[pl.ds(0, FACE, stride=4), :]
        high = src[pl.ds(3, FACE, stride=4), :]
        near = jnp.where(span == 0, pltpu.roll(high, LANES - 24, 1), pltpu.roll(high, 8, 1))
        to_operand(NODES + 4 * FACE, near - low)
        near = jnp.where(span == 3, pltpu.roll(low, 24, 1), pltpu.roll(low, LANES - 8, 1))
        to_operand(NODES + 5 * FACE, near - high)

    def y_jumps(src, r):
        for side in (2, 3):
            @pl.when(y_sends[r][side - 2])
            def _():
                arrival(r, side).wait_recv()
        for e in range(4):
            rows = slice(40 * e, 40 * e + 40)
            low, high = y_block(src, e, 0), y_block(src, e, 1)
            far = ry[r, 0]
            if e:
                far = pltpu.roll(far, LANES - 32 * e, 1)
            jump[rows, :] = jnp.where(quarter == 0, far, pltpu.roll(high, 32, 1)) - low
            far = ry[r, 1]
            if e < 3:
                far = pltpu.roll(far, 96 - 32 * e, 1)
            rows = slice(FACE + 40 * e, FACE + 40 * e + 40)
            jump[rows, :] = jnp.where(quarter == 3, far, pltpu.roll(low, LANES - 32, 1)) - high
        to_operand(NODES + 2 * FACE, jump[...])

    def operate_own(src):
        to_operand(0, scale_lane * src[...])
        span_jumps(src)
        products([(0, NODES), (NODES + 4 * FACE, KDIM)], begin)

    def operate_rest(src):
        products(FACE_ROWS, add)
        acc[...] = acc[...] - dt[...] * src[...]

    loads[3].wait()
    scale_lane = jnp.zeros((1, LANES), f32)
    for s in range(16):
        scale_lane = jnp.where(slot_of == s, scale[s], scale_lane)

    def turn(source, column):
        high, low = split(source.T)
        wh[:, column : column + source.shape[0]] = high
        wl[:, column : column + source.shape[0]] = low

    loads[4].wait()
    for block in range(5):
        turn(vol[block * 128 : block * 128 + 128, :], block * 128)
    loads[5].wait()
    for b in range(5):
        columns = slice(b * 128, b * 128 + 128)
        lfy[b] = lft[2 * FACE : 4 * FACE, columns]
        for high in range(2):
            for e in range(4):
                row = 2 * FACE + high * FACE + 40 * e
                lft[row : row + 40, columns] = lfy[b, pl.ds(high * FACE + e, 40, stride=4), :]
    for block in range(7):
        turn(lft[block * 128 : block * 128 + 128, :], NODES + block * 128)
    turn(lft[896:960, :], NODES + 896)

    loads[6].wait()
    spread16 = jnp.where(iota((16, LANES), 0) == slot_of, 1.0, 0.0).astype(bf16)
    rest = dmp[...]
    total = jnp.zeros((NODES, LANES), f32)
    for _ in range(3):
        piece = rest.astype(bf16)
        rest = rest - piece.astype(f32)
        total = total + lax.dot_general(
            piece, spread16, (((0,), (0,)), ((), ())), preferred_element_type=f32
        )
    dt[...] = total

    loads[7].wait()
    loads[8].wait()
    f00, f01, f10, f11 = part(0, 0), part(0, 1), part(1, 0), part(1, 1)

    def forcing_at(moment):
        a, b = omegas[0] * moment, omegas[1] * moment
        return (
            f00 * math.cos(a) - f01 * math.sin(a) + f10 * math.cos(b) - f11 * math.sin(b)
        )

    f1[...] = forcing_at(h)
    f2[...] = forcing_at(2 * h)

    operate_own(st)
    pl.semaphore_wait(barrier, expected)
    for side in range(2):
        send_x(0, side, st, near_side[side])
    send_y(0, st)
    for side in range(2):
        send_x(0, side, st, far_side[side])
    y_jumps(st, 0)
    for side in range(2):
        @pl.when(near_side[side])
        def _():
            arrival(0, side).wait_recv()

        @pl.when(far_side[side])
        def _():
            set_x(side, -face(st, side))

        @pl.when(jnp.logical_not(far_side[side]))
        def _():
            set_x(side, rx[0, side] - face(st, side))

    operate_rest(st)
    st[...] = 0.5 * h * (k1[...] + acc[...] + f1[...])


    def damping_copy(side):
        return pltpu.make_async_remote_copy(
            src_ref=sd, dst_ref=rd, send_sem=ssd.at[0], recv_sem=rsd.at[0],
            device_id=sides[side][1], device_id_type=MESH,
        )

    @pl.when(far_any)
    def _():
        send_y(1, st)
        for side in range(2):
            send_x(1, side, st)
        operate_own(st)
        y_jumps(st, 1)
        for side in range(2):
            @pl.when(far_side[side])
            def _():
                set_x(side, -face(st, side))
                arrival(2, 1 - side).wait_recv()
                set_x(1 - side, rx[2, 1 - side] - face(st, 1 - side))

        operate_rest(st)
        k1[...] = st[...] + h * (acc[...] + f1[...])

        for side in range(2):
            @pl.when(far_side[side])
            def _():
                set_x(side, jnp.zeros((FACE, LANES), f32))
                set_x(1 - side, sx[0, side])
                mine_damped = face(dt, side)
                packed = [jnp.zeros((16, LANES), f32), jnp.zeros((16, LANES), f32)]
                for b in range(10):
                    piece = mine_damped[16 * b : 16 * b + 16]
                    packed[b // 8] = jnp.where((lane & 7) == b % 8, piece, packed[b // 8])
                sd[0:16, :] = packed[0]
                sd[16:32, :] = packed[1]
                sd[32:, :] = jnp.broadcast_to(scale_lane, (8, LANES))

        products(X_ROWS, ghost_value)
        send_y(5, gst)
        for side in range(2):
            @pl.when(far_side[side])
            def _():
                arrival(0, side).wait_recv()
                set_x(side, rx[0, side])
                set_x(1 - side, jnp.zeros((FACE, LANES), f32))

        products(X_ROWS, far_value)

    send_y(2, st)
    for side in range(2):
        send_x(2, side, st)
    for side in range(2):
        send_x(3, side, k1)

        @pl.when(far_side[side])
        def _():
            damping_copy(side).start()

    q1[...] = st[...]

    def keep_state(n, value):
        lanes = slice(n * LANES, n * LANES + LANES)
        high, low = split(value)
        qh[:, lanes] = high
        ql[:, lanes] = low
        high, low = split(value.T)
        th[lanes, :] = high
        tl[lanes, :] = low

    @pl.when(far_any)
    def _():
        to_operand(0, gst[...])
        span_jumps(gst)
        y_jumps(gst, 5)
        for side in range(2):
            set_x(side, -face(gst, side))
        for side in range(2):
            @pl.when(far_side[side])
            def _():
                other = 1 - side
                corr[0] = face(gst, other)
                corr[1] = face_products(other, [(0, NODES)])
                corr[2] = face_products(other, [(NODES, KDIM)])

    operate_own(st)
    y_jumps(st, 2)
    for side in range(2):
        @pl.when(jnp.logical_and(near_side[side], jnp.logical_not(far_any)))
        def _():
            arrival(2, side).wait_recv()

        @pl.when(far_side[side])
        def _():
            arrival(1, side).wait_recv()
            set_x(side, rx[1, side] + corr[0] - face(st, side))

        @pl.when(jnp.logical_not(far_side[side]))
        def _():
            set_x(side, rx[2, side] - face(st, side))

    operate_rest(st)
    k1[...] = acc[...] + f1[...]
    st[...] = q1[...] + h * k1[...]
    send_y(4, st)
    for side in range(2):
        send_x(4, side, st)
    operate_own(st)
    keep_state(0, q1[...])

    for side in range(2):
        @pl.when(far_side[side])
        def _():
            other = 1 - side
            set_x(side, jnp.zeros((FACE, LANES), f32))
            set_x(other, face(q1, side))
            direct = face_products(other, X_ROWS)
            damping_copy(side).wait_recv()
            damped = []
            for b in range(10):
                piece = rd[16 * (b // 8) : 16 * (b // 8) + 16, :]
                piece = jnp.where((lane & 7) == b % 8, piece, 0.0)
                if b % 8:
                    piece = pltpu.roll(piece, LANES - b % 8, 1)
                for shift in (1, 2, 4):
                    piece = piece + pltpu.roll(piece, shift, 1)
                damped.append(piece)
            damped = jnp.concatenate(damped, axis=0)
            change = rd[32:33, :] * corr[1] + corr[2] - damped * corr[0] + direct
            corr[0] = corr[0] + h * change

    y_jumps(st, 4)
    for side in range(2):
        @pl.when(near_side[side])
        def _():
            arrival(4, side).wait_recv()

        @pl.when(far_side[side])
        def _():
            arrival(3, side).wait_recv()
            set_x(side, rx[3, side] + corr[0] - face(st, side))

        @pl.when(jnp.logical_not(far_side[side]))
        def _():
            set_x(side, rx[4, side] - face(st, side))

    operate_rest(st)
    keep_state(1, q1[...] + 0.5 * h * (k1[...] + acc[...] + f2[...]))
    results = [
        pltpu.make_async_copy(th, qh_out, out_sem.at[0]),
        pltpu.make_async_copy(tl, ql_out, out_sem.at[1]),
    ]
    for result in results:
        result.start()

    pairs = mm(th[...], qh[...]) + (mm(th[...], ql[...]) + mm(tl[...], qh[...])) + mm(tl[...], ql[...])
    row = iota((2 * LANES, 2 * LANES), 0)
    col = iota((2 * LANES, 2 * LANES), 1)
    pairs = jnp.where(((row >> 3) & 15) == ((col >> 3) & 15), pairs, 0.0)
    sums = jnp.sum(pairs.reshape(2, 16, 8, 2 * LANES), axis=1)
    halves = []
    for half in range(2):
        value = sums[:, :, half * LANES : half * LANES + LANES].reshape(16, LANES)
        for shift in (64, 32, 16, 8):
            value = value + pltpu.roll(value, shift, 1)
        halves.append(value)
    both = jnp.where((lane & 8) == 0, halves[0], halves[1])
    sub = iota((8, LANES), 0)
    wide = iota((8, LANES), 1)
    for t in range(2):
        picked = jnp.where((wide >> 4) == sub, both[8 * t : 8 * t + 8], 0.0)
        zs[0, t : t + 1, :] = jnp.sum(picked, axis=0, keepdims=True)

    for phase in range(2):
        copies = []
        for k in range(1, GROUP):
            copy = pltpu.make_async_remote_copy(
                src_ref=zs.at[phase],
                dst_ref=zr.at[phase, mine[phase]],
                send_sem=ssz.at[phase, k],
                recv_sem=rsz.at[phase, mine[phase]],
                device_id=partner(phase, k),
                device_id_type=MESH,
            )
            copy.start()
            copies.append(copy)
        zr[phase, mine[phase]] = zs[phase]
        for k in range(1, GROUP):
            source = (mine[phase] + k) % GROUP
            pltpu.make_async_remote_copy(
                src_ref=zs.at[phase],
                dst_ref=zr.at[phase, source],
                send_sem=ssz.at[phase, k],
                recv_sem=rsz.at[phase, source],
                device_id=partner(phase, k),
                device_id_type=MESH,
            ).wait_recv()
        total = zr[phase, 0]
        for s in range(1, GROUP):
            total = total + zr[phase, s]
        if phase == 0:
            zs[1] = total
        else:
            gram_out[...] = total
        for copy in copies:
            copy.wait_send()

    for r, sent in enumerate(x_sends):
        for side in range(2):
            @pl.when(sent[side])
            def _():
                copy_to(r, side).wait_send()
    for r, sent in enumerate(y_sends):
        for side in range(2 if sent else 0):
            @pl.when(sent[side])
            def _():
                copy_to(r, 2 + side).wait_send()
    for side in range(2):
        @pl.when(far_side[side])
        def _():
            damping_copy(side).wait_send()

    for result in results:
        result.wait()


def finish_kernel(
    unknowns, qh_hbm, ql_hbm, gram, slots_hbm, basis_out, factor_out,
    slots, qh, ql, stage, factor, load_sem, sems, factor_sem,
):
    loads = [
        pltpu.make_async_copy(slots_hbm, slots, load_sem.at[0]),
        pltpu.make_async_copy(qh_hbm, qh, load_sem.at[1]),
        pltpu.make_async_copy(ql_hbm, ql, load_sem.at[2]),
    ]
    for load in loads:
        load.start()
    sub = iota((8, LANES), 0)
    lane = iota((8, LANES), 1)
    tiles = []
    for t in range(2):
        value = jnp.where((lane >> 4) == sub, gram[t : t + 1, :], 0.0)
        for shift in (64, 32, 16):
            value = value + pltpu.roll(value, shift, 1)
        tiles.append(value)
    low = (lane & 8) == 0
    a11 = jnp.where(low, tiles[0], pltpu.roll(tiles[0], 8, 1))
    a12 = jnp.where(low, pltpu.roll(tiles[0], LANES - 8, 1), tiles[0])
    a21 = jnp.where(low, tiles[1], pltpu.roll(tiles[1], 8, 1))
    a22 = jnp.where(low, pltpu.roll(tiles[1], LANES - 8, 1), tiles[1])
    root = math.sqrt(unknowns)
    h = step_size
    work = []
    for w in range(2):
        angle = omegas[w] * h
        work.append([
            a11 + a22 + math.cos(angle) * (a12 + a21),
            math.sin(angle) * (a21 - a12),
            jnp.where((lane & 7) == sub, 1.0, 0.0),
            jnp.zeros((8, LANES), f32),
        ])
    for i in range(8):
        below, here = sub > i, sub == i
        for w in range(2):
            g_re, g_im, m_re, m_im = work[w]
            c_re = jnp.sum(jnp.where(lane == i, g_re, 0.0), axis=1, keepdims=True)
            c_im = jnp.sum(jnp.where(lane == i, g_im, 0.0), axis=1, keepdims=True)
            pivot = c_re[i : i + 1, :]
            inverse = 1.0 / jnp.sqrt(pivot)
            c_re = c_re / pivot
            c_im = c_im / pivot

            def update(re, im):
                r_re, r_im = re[i : i + 1, :], im[i : i + 1, :]
                new_re = re - (c_re * r_re - c_im * r_im)
                new_im = im - (c_re * r_im + c_im * r_re)
                return (
                    jnp.where(below, new_re, jnp.where(here, re * inverse, re)),
                    jnp.where(below, new_im, jnp.where(here, im * inverse, im)),
                )

            g_re, g_im = update(g_re, g_im)
            m_re, m_im = update(m_re, m_im)
            work[w] = [g_re, g_im, m_re, m_im]
    for w in range(2):
        g_re, g_im = work[w][:2]
        factor[w, 0] = jnp.where(lane >= sub, g_re * (h / root), 0.0)[:, :8]
        factor[w, 1] = jnp.where(lane > sub, g_im * (h / root), 0.0)[:, :8]
    copies = [pltpu.make_async_copy(factor, factor_out, factor_sem)]
    copies[0].start()
    for load in loads:
        load.wait()
    keep = (iota((LANES, LANES), 0) & 15) == lane_slots(slots)
    q_high, q_low = qh[...], ql[...]
    for w in range(2):
        m_re, m_im = work[w][2:]
        for p in range(2):
            blocks = []
            for n in range(2):
                c, s = math.cos(omegas[w] * h * (n + 1)), math.sin(omegas[w] * h * (n + 1))
                if p == 0:
                    coef = root * (c * m_re - s * m_im)
                else:
                    coef = -root * (s * m_re + c * m_im)
                coef = jnp.broadcast_to(coef[:, None, :], (8, 16, LANES)).reshape(LANES, LANES)
                blocks.append(jnp.where(keep, coef, 0.0))
            high, low_part = split(jnp.concatenate(blocks, axis=1))
            result = mm(high, q_high) + (mm(high, q_low) + mm(low_part, q_high))
            stage[w, p] = result.reshape(8, 16, NODES)
            copy = pltpu.make_async_copy(stage.at[w, p], basis_out.at[w, p], sems.at[w, p])
            copy.start()
            copies.append(copy)
    for copy in copies:
        copy.wait()


def on_device(forcing, scale, damping, volume, lift, slots):
    hbm = pl.BlockSpec(memory_space=pltpu.HBM)
    vmem = pl.BlockSpec(memory_space=pltpu.VMEM)
    state = pltpu.VMEM((NODES, LANES), f32)
    q_high, q_low, gram = pl.pallas_call(
        march_kernel,
        out_shape=(
            jax.ShapeDtypeStruct((2 * LANES, NODES), bf16),
            jax.ShapeDtypeStruct((2 * LANES, NODES), bf16),
            jax.ShapeDtypeStruct((2, LANES), f32),
        ),
        in_specs=[hbm] * 6,
        out_specs=(hbm, hbm, vmem),
        scratch_shapes=[
            pltpu.SMEM(slots.shape, jnp.int32),
            pltpu.SMEM(scale.shape, f32),
            pltpu.VMEM(forcing.shape, bf16),
            pltpu.VMEM((NODES, NODES), f32),
            pltpu.VMEM((6 * FACE, NODES), f32),
            pltpu.VMEM((5, 2 * FACE, LANES), f32),
            pltpu.VMEM((16, NODES), f32),
            pltpu.VMEM((NODES, KDIM), bf16),
            pltpu.VMEM((NODES, KDIM), bf16),
            state, state, state, state, state, state,
            pltpu.VMEM((2 * FACE, LANES), f32),
            pltpu.VMEM((KDIM, 2 * LANES), bf16),
            state,
            pltpu.VMEM((NODES, 2 * LANES), bf16),
            pltpu.VMEM((NODES, 2 * LANES), bf16),
            pltpu.VMEM((2 * LANES, NODES), bf16),
            pltpu.VMEM((2 * LANES, NODES), bf16),
            pltpu.VMEM((3, FACE, LANES), f32),
            state,
            pltpu.VMEM((40, LANES), f32),
            pltpu.VMEM((40, LANES), f32),
            pltpu.VMEM((5, 2, FACE, LANES), f32),
            pltpu.VMEM((6, 2, 40, LANES), f32),
            pltpu.VMEM((5, 2, FACE, LANES), f32),
            pltpu.VMEM((6, 2, 40, LANES), f32),
            pltpu.VMEM((2, 2, LANES), f32),
            pltpu.VMEM((2, GROUP, 2, LANES), f32),
            pltpu.SemaphoreType.DMA((9,)),
            pltpu.SemaphoreType.DMA((5, 2)),
            pltpu.SemaphoreType.DMA((5, 2)),
            pltpu.SemaphoreType.DMA((6, 2)),
            pltpu.SemaphoreType.DMA((6, 2)),
            pltpu.SemaphoreType.DMA((1,)),
            pltpu.SemaphoreType.DMA((1,)),
            pltpu.SemaphoreType.DMA((2, GROUP)),
            pltpu.SemaphoreType.DMA((2, GROUP)),
            pltpu.SemaphoreType.DMA((2,)),
        ],
        compiler_params=pltpu.CompilerParams(
            collective_id=0, has_side_effects=True, vmem_limit_bytes=64 * 1024 * 1024
        ),
        name="march",
    )(forcing, scale, damping, volume, lift, slots)
    unknowns = forcing.shape[3] * NODES * lax.axis_size("gx") * lax.axis_size("gy")
    shape = forcing.shape
    return pl.pallas_call(
        lambda *refs: finish_kernel(unknowns, *refs),
        out_shape=(
            jax.ShapeDtypeStruct(shape, f32),
            jax.ShapeDtypeStruct((2, 2, 8, 8), f32),
        ),
        in_specs=[hbm, hbm, vmem, hbm],
        out_specs=(hbm, hbm),
        scratch_shapes=[
            pltpu.SMEM(slots.shape, jnp.int32),
            pltpu.VMEM((2 * LANES, NODES), bf16),
            pltpu.VMEM((2 * LANES, NODES), bf16),
            pltpu.VMEM(shape, f32),
            pltpu.VMEM((2, 2, 8, 8), f32),
            pltpu.SemaphoreType.DMA((3,)),
            pltpu.SemaphoreType.DMA((2, 2)),
            pltpu.SemaphoreType.DMA,
        ],
        compiler_params=pltpu.CompilerParams(vmem_limit_bytes=64 * 1024 * 1024),
        name="finish",
    )(q_high, q_low, gram, slots)


def solution(mesh):
    placed = (
        P(None, None, None, ("gx", "gy"), None),
        P(("gx", "gy")),
        P(("gx", "gy"), None),
        P(),
        P(),
        P("gx", "gy", None),
    )
    return jax.shard_map(
        on_device,
        mesh=mesh,
        in_specs=placed,
        out_specs=(P(None, None, None, ("gx", "gy"), None), P()),
        check_vma=False,
    )
```

```python
import math

import jax
import jax.numpy as jnp
from jax import lax
from jax.experimental import pallas as pl
from jax.experimental.pallas import tpu as pltpu
from jax.sharding import PartitionSpec as P

NODES = 640
FACE = 160
LANES = 128
KDIM = NODES + 6 * FACE
step_size = 0.4
omegas = (1.3, 3.1)
MESH = pl.DeviceIdType.MESH
f32 = jnp.float32
bf16 = jnp.bfloat16
GROUP = 16


def iota(shape, dim):
    return lax.broadcasted_iota(jnp.int32, shape, dim)


def split(value):
    high = value.astype(bf16)
    return high, (value - high.astype(f32)).astype(bf16)


def mm(left, right):
    return lax.dot_general(left, right, (((1,), (0,)), ((), ())), preferred_element_type=f32)


def lane_slots(slots_ref):
    group = iota((1, LANES), 1) >> 3
    result = jnp.zeros((1, LANES), jnp.int32)
    for g in range(16):
        result = jnp.where(group == g, slots_ref[0, g // 4, g % 4], result)
    return result


def placement(slots_ref):
    row = iota((LANES, LANES), 0)
    lane = iota((LANES, LANES), 1)
    return ((row >> 4) == (lane & 7)) & ((row & 15) == lane_slots(slots_ref))


def march_kernel(
    forcing, scale_hbm, damping, volume, lift, slots_hbm,
    qh_out, ql_out, gram_out,
    slots, scale, fb, vol, lft, lfy, dmp, wh, wl, f1, f2, st, q1, k1, dt, jump, xb, acc,
    qh, ql, th, tl, corr, gst, sd, rd,
    sx, sy, rx, ry, zs, zr,
    load_sem, ssx, rsx, ssy, rsy, ssd, rsd, ssz, rsz, out_sem,
):
    gx, gy = lax.axis_index("gx"), lax.axis_index("gy")
    last_x, last_y = lax.axis_size("gx") - 1, lax.axis_size("gy") - 1
    h = step_size

    pairs = [
        (slots_hbm, slots),
        (forcing.at[0, 0], fb.at[0, 0]),
        (forcing.at[1, 0], fb.at[1, 0]),
        (scale_hbm, scale),
        (volume, vol),
        (lift, lft),
        (damping, dmp),
        (forcing.at[0, 1], fb.at[0, 1]),
        (forcing.at[1, 1], fb.at[1, 1]),
    ]
    loads = [
        pltpu.make_async_copy(source, target, load_sem.at[n])
        for n, (source, target) in enumerate(pairs)
    ]

    sides = [
        (gx > 0, (gx - 1, gy)),
        (gx < last_x, (gx + 1, gy)),
        (gy > 0, (gx, gy - 1)),
        (gy < last_y, (gx, gy + 1)),
    ]
    yy, zh, xx = gx // 8, (gx // 4) % 2, gx % 4
    mine = [zh * 8 + gy, yy * 4 + xx]

    def partner(phase, k):
        p = (mine[phase] + k) % GROUP
        if phase == 0:
            return (yy * 8 + (p // 8) * 4 + xx, p % 8)
        return ((p // 4) * 8 + zh * 4 + p % 4, gy)

    far_side = [
        jnp.logical_and(gx > 0, xx == 0),
        jnp.logical_and(gx < last_x, xx == 3),
    ]

    far_any = jnp.logical_or(far_side[0], far_side[1])
    near_side = [
        jnp.logical_and(sides[n][0], jnp.logical_not(far_side[n])) for n in range(2)
    ]
    far_y = [jnp.logical_and(sides[2 + n][0], far_any) for n in range(2)]
    all_x, all_y = [sides[0][0], sides[1][0]], [sides[2][0], sides[3][0]]
    x_sends = [all_x, far_side, near_side, far_side, near_side]
    y_sends = [all_y, far_y, all_y, [], all_y, far_y]

    barrier = pltpu.get_barrier_semaphore()
    expected = 2 * (GROUP - 1)
    for there, place in sides:
        expected = expected + there.astype(jnp.int32)

        @pl.when(there)
        def _():
            pl.semaphore_signal(barrier, inc=1, device_id=place, device_id_type=MESH)

    for load in loads:
        load.start()
    for phase in range(2):
        for k in range(1, GROUP):
            pl.semaphore_signal(
                barrier, inc=1, device_id=partner(phase, k), device_id_type=MESH
            )

    for side in range(4):
        land = rx if side < 2 else ry

        @pl.when(jnp.logical_not(sides[side][0]))
        def _():
            for r in range(land.shape[0]):
                land[r, side % 2] = jnp.zeros(land.shape[2:], f32)

    loads[0].wait()
    one_hot = placement(slots).astype(f32).astype(bf16)
    slot_of = lane_slots(slots)

    def part(w, p):
        rows = fb[w, p].reshape(LANES, NODES)
        return lax.dot_general(rows, one_hot, (((0,), (0,)), ((), ())), preferred_element_type=f32)

    loads[1].wait()
    loads[2].wait()
    f00, f10 = part(0, 0), part(1, 0)
    k1[...] = f00 + f10
    st[...] = h * k1[...]

    lane = iota((1, LANES), 1)
    quarter = lane >> 5
    span = (lane >> 3) & 3

    def copy_to(r, side):
        out, land = (sx, rx) if side < 2 else (sy, ry)
        s_sem, r_sem = (ssx, rsx) if side < 2 else (ssy, rsy)
        return pltpu.make_async_remote_copy(
            src_ref=out.at[r, side % 2],
            dst_ref=land.at[r, 1 - side % 2],
            send_sem=s_sem.at[r, side % 2],
            recv_sem=r_sem.at[r, 1 - side % 2],
            device_id=sides[side][1],
            device_id_type=MESH,
        )

    def arrival(r, side):
        out, land = (sx, rx) if side < 2 else (sy, ry)
        s_sem, r_sem = (ssx, rsx) if side < 2 else (ssy, rsy)
        return pltpu.make_async_remote_copy(
            src_ref=out.at[r, side % 2],
            dst_ref=land.at[r, side % 2],
            send_sem=s_sem.at[r, side % 2],
            recv_sem=r_sem.at[r, side % 2],
            device_id=sides[side][1],
            device_id_type=MESH,
        )

    def y_block(src, e, high):
        return src[pl.ds((12 if high else 0) + e, 40, stride=16), :]

    def face(src, side):
        start = 48 if side else 0
        return src[...].reshape(10, 64, LANES)[:, start : start + 16].reshape(FACE, LANES)

    def send_x(r, side, src, when=None):
        @pl.when(x_sends[r][side] if when is None else when)
        def _():
            sx[r, side] = face(src, side)
            copy_to(r, side).start()

    def send_y(r, src):
        for high in range(2):
            packed = jnp.zeros((40, LANES), f32)
            for e in range(4):
                shift = (32 * e - (96 if high else 0)) % LANES
                block = y_block(src, e, high)
                if shift:
                    block = pltpu.roll(block, shift, 1)
                packed = jnp.where(quarter == e, block, packed)

            @pl.when(y_sends[r][high])
            def _():
                sy[r, high] = packed
                copy_to(r, 2 + high).start()

    def to_operand(row, value):
        high, low = split(value)
        rows = pl.ds(row, value.shape[0])
        xb[rows, 0:LANES] = high
        xb[rows, LANES:] = low

    def products(ranges, done):
        for block in range(5):
            rows = slice(block * 128, block * 128 + 128)
            both = None
            for lo, hi in ranges:
                wide = mm(wh[rows, lo:hi], xb[lo:hi, :])
                term = wide[:, :LANES] + wide[:, LANES:] + mm(wl[rows, lo:hi], xb[lo:hi, :LANES])
                both = term if both is None else both + term
            done(rows, both)

    def begin(rows, value):
        acc[rows, :] = value

    def add(rows, value):
        acc[rows, :] = acc[rows, :] + value

    def far_value(rows, value):
        st[rows, :] = st[rows, :] + 0.5 * h * value

    def ghost_value(rows, value):
        gst[rows, :] = 0.5 * h * value

    X_ROWS = [(NODES, NODES + 2 * FACE)]
    OWN_ROWS = [(0, NODES), (NODES + 4 * FACE, KDIM)]
    FACE_ROWS = [(NODES, NODES + 4 * FACE)]

    def face_products(side, ranges):
        start = 48 if side else 0
        rows = [slice(64 * f + start, 64 * f + start + 16) for f in range(10)]
        total = None
        for lo, hi in ranges:
            left_high = jnp.concatenate([wh[r, lo:hi] for r in rows], axis=0)
            left_low = jnp.concatenate([wl[r, lo:hi] for r in rows], axis=0)
            wide = mm(left_high, xb[lo:hi, :])
            value = wide[:, :LANES] + wide[:, LANES:] + mm(left_low, xb[lo:hi, :LANES])
            total = value if total is None else total + value
        return total

    def set_x(side, value):
        to_operand(NODES + side * FACE, value)

    def span_jumps(src):
        low = src[pl.ds(0, FACE, stride=4), :]
        high = src[pl.ds(3, FACE, stride=4), :]
        near = jnp.where(span == 0, pltpu.roll(high, LANES - 24, 1), pltpu.roll(high, 8, 1))
        to_operand(NODES + 4 * FACE, near - low)
        near = jnp.where(span == 3, pltpu.roll(low, 24, 1), pltpu.roll(low, LANES - 8, 1))
        to_operand(NODES + 5 * FACE, near - high)

    def y_jumps(src, r):
        for side in (2, 3):
            @pl.when(y_sends[r][side - 2])
            def _():
                arrival(r, side).wait_recv()
        for e in range(4):
            rows = slice(40 * e, 40 * e + 40)
            low, high = y_block(src, e, 0), y_block(src, e, 1)
            far = ry[r, 0]
            if e:
                far = pltpu.roll(far, LANES - 32 * e, 1)
            jump[rows, :] = jnp.where(quarter == 0, far, pltpu.roll(high, 32, 1)) - low
            far = ry[r, 1]
            if e < 3:
                far = pltpu.roll(far, 96 - 32 * e, 1)
            rows = slice(FACE + 40 * e, FACE + 40 * e + 40)
            jump[rows, :] = jnp.where(quarter == 3, far, pltpu.roll(low, LANES - 32, 1)) - high
        to_operand(NODES + 2 * FACE, jump[...])

    def operate_own(src):
        to_operand(0, scale_lane * src[...])
        span_jumps(src)
        products(OWN_ROWS, begin)

    def operate_rest(src):
        products(FACE_ROWS, add)
        acc[...] = acc[...] - dt[...] * src[...]

    loads[3].wait()
    scale_lane = jnp.zeros((1, LANES), f32)
    for s in range(16):
        scale_lane = jnp.where(slot_of == s, scale[s], scale_lane)

    def turn(source, column):
        high, low = split(source.T)
        wh[:, column : column + source.shape[0]] = high
        wl[:, column : column + source.shape[0]] = low

    loads[4].wait()
    for block in range(5):
        turn(vol[block * 128 : block * 128 + 128, :], block * 128)
    loads[5].wait()
    for b in range(5):
        columns = slice(b * 128, b * 128 + 128)
        lfy[b] = lft[2 * FACE : 4 * FACE, columns]
        for high in range(2):
            for e in range(4):
                row = 2 * FACE + high * FACE + 40 * e
                lft[row : row + 40, columns] = lfy[b, pl.ds(high * FACE + e, 40, stride=4), :]
    for block in range(7):
        turn(lft[block * 128 : block * 128 + 128, :], NODES + block * 128)
    turn(lft[896:960, :], NODES + 896)

    loads[6].wait()
    spread16 = jnp.where(iota((16, LANES), 0) == slot_of, 1.0, 0.0).astype(bf16)
    rest = dmp[...]
    total = jnp.zeros((NODES, LANES), f32)
    for _ in range(3):
        piece = rest.astype(bf16)
        rest = rest - piece.astype(f32)
        total = total + lax.dot_general(
            piece, spread16, (((0,), (0,)), ((), ())), preferred_element_type=f32
        )
    dt[...] = total

    loads[7].wait()
    loads[8].wait()
    f00, f01, f10, f11 = part(0, 0), part(0, 1), part(1, 0), part(1, 1)

    def forcing_at(moment):
        a, b = omegas[0] * moment, omegas[1] * moment
        return (
            f00 * math.cos(a) - f01 * math.sin(a) + f10 * math.cos(b) - f11 * math.sin(b)
        )

    f1[...] = forcing_at(h)
    f2[...] = forcing_at(2 * h)

    operate_own(st)
    pl.semaphore_wait(barrier, expected)
    for side in range(2):
        send_x(0, side, st, near_side[side])
    send_y(0, st)
    for side in range(2):
        send_x(0, side, st, far_side[side])
    y_jumps(st, 0)
    for side in range(2):
        @pl.when(near_side[side])
        def _():
            arrival(0, side).wait_recv()

        @pl.when(far_side[side])
        def _():
            set_x(side, -face(st, side))

        @pl.when(jnp.logical_not(far_side[side]))
        def _():
            set_x(side, rx[0, side] - face(st, side))

    operate_rest(st)
    st[...] = 0.5 * h * (k1[...] + acc[...] + f1[...])


    def damping_copy(side):
        return pltpu.make_async_remote_copy(
            src_ref=sd, dst_ref=rd, send_sem=ssd.at[0], recv_sem=rsd.at[0],
            device_id=sides[side][1], device_id_type=MESH,
        )

    @pl.when(far_any)
    def _():
        send_y(1, st)
        for side in range(2):
            send_x(1, side, st)
        to_operand(0, scale_lane * st[...])
        span_jumps(st)
        for side in range(2):
            @pl.when(far_side[side])
            def _():
                set_x(side, -face(st, side))
                corr[1] = face_products(side, OWN_ROWS)

        y_jumps(st, 1)
        for side in range(2):
            @pl.when(far_side[side])
            def _():
                arrival(2, 1 - side).wait_recv()
                set_x(1 - side, rx[2, 1 - side] - face(st, 1 - side))
                slope = corr[1] + face_products(side, FACE_ROWS)
                slope = slope - face(dt, side) * face(st, side) + face(f1, side)
                sx[3, side] = face(st, side) + h * slope

        for side in range(2):
            @pl.when(far_side[side])
            def _():
                set_x(side, jnp.zeros((FACE, LANES), f32))
                set_x(1 - side, sx[0, side])
                mine_damped = face(dt, side)
                packed = [jnp.zeros((16, LANES), f32), jnp.zeros((16, LANES), f32)]
                for b in range(10):
                    piece = mine_damped[16 * b : 16 * b + 16]
                    packed[b // 8] = jnp.where((lane & 7) == b % 8, piece, packed[b // 8])
                sd[0:16, :] = packed[0]
                sd[16:32, :] = packed[1]
                sd[32:, :] = jnp.broadcast_to(scale_lane, (8, LANES))

        products(X_ROWS, ghost_value)
        send_y(5, gst)
        for side in range(2):
            @pl.when(far_side[side])
            def _():
                arrival(0, side).wait_recv()
                set_x(side, rx[0, side])
                set_x(1 - side, jnp.zeros((FACE, LANES), f32))
                inner = face_products(1 - side, X_ROWS)
                sx[2, 1 - side] = face(st, 1 - side) + 0.5 * h * inner
                copy_to(2, 1 - side).start()

        products(X_ROWS, far_value)

    send_y(2, st)
    for side in range(2):
        send_x(2, side, st, jnp.logical_and(near_side[side], jnp.logical_not(far_any)))
    for side in range(2):
        @pl.when(far_side[side])
        def _():
            copy_to(3, side).start()
            damping_copy(side).start()

    q1[...] = st[...]

    def keep_state(n, value):
        lanes = slice(n * LANES, n * LANES + LANES)
        high, low = split(value)
        qh[:, lanes] = high
        ql[:, lanes] = low
        high, low = split(value.T)
        th[lanes, :] = high
        tl[lanes, :] = low

    @pl.when(far_any)
    def _():
        to_operand(0, gst[...])
        span_jumps(gst)
        y_jumps(gst, 5)
        for side in range(2):
            set_x(side, -face(gst, side))
        for side in range(2):
            @pl.when(far_side[side])
            def _():
                other = 1 - side
                corr[0] = face(gst, other)
                corr[1] = face_products(other, [(0, NODES)])
                corr[2] = face_products(other, [(NODES, KDIM)])

    operate_own(st)
    y_jumps(st, 2)
    for side in range(2):
        @pl.when(jnp.logical_and(near_side[side], jnp.logical_not(far_any)))
        def _():
            arrival(2, side).wait_recv()

        @pl.when(far_side[side])
        def _():
            arrival(1, side).wait_recv()
            set_x(side, rx[1, side] + corr[0] - face(st, side))

        @pl.when(jnp.logical_not(far_side[side]))
        def _():
            set_x(side, rx[2, side] - face(st, side))

    for side in range(2):
        @pl.when(near_side[side])
        def _():
            slope = face(acc, side) + face_products(side, FACE_ROWS)
            slope = slope - face(dt, side) * face(st, side) + face(f1, side)
            sx[4, side] = face(q1, side) + h * slope
            copy_to(4, side).start()

    operate_rest(st)
    k1[...] = acc[...] + f1[...]
    st[...] = q1[...] + h * k1[...]
    send_y(4, st)
    operate_own(st)
    keep_state(0, q1[...])

    for side in range(2):
        @pl.when(far_side[side])
        def _():
            other = 1 - side
            set_x(side, jnp.zeros((FACE, LANES), f32))
            set_x(other, face(q1, side))
            direct = face_products(other, X_ROWS)
            damping_copy(side).wait_recv()
            damped = []
            for b in range(10):
                piece = rd[16 * (b // 8) : 16 * (b // 8) + 16, :]
                piece = jnp.where((lane & 7) == b % 8, piece, 0.0)
                if b % 8:
                    piece = pltpu.roll(piece, LANES - b % 8, 1)
                for shift in (1, 2, 4):
                    piece = piece + pltpu.roll(piece, shift, 1)
                damped.append(piece)
            damped = jnp.concatenate(damped, axis=0)
            change = rd[32:33, :] * corr[1] + corr[2] - damped * corr[0] + direct
            corr[0] = corr[0] + h * change

    y_jumps(st, 4)
    for side in range(2):
        @pl.when(near_side[side])
        def _():
            arrival(4, side).wait_recv()

        @pl.when(far_side[side])
        def _():
            arrival(3, side).wait_recv()
            set_x(side, rx[3, side] + corr[0] - face(st, side))

        @pl.when(jnp.logical_not(far_side[side]))
        def _():
            set_x(side, rx[4, side] - face(st, side))

    operate_rest(st)
    keep_state(1, q1[...] + 0.5 * h * (k1[...] + acc[...] + f2[...]))
    results = [
        pltpu.make_async_copy(th, qh_out, out_sem.at[0]),
        pltpu.make_async_copy(tl, ql_out, out_sem.at[1]),
    ]
    for result in results:
        result.start()

    pairs = mm(th[...], qh[...]) + (mm(th[...], ql[...]) + mm(tl[...], qh[...])) + mm(tl[...], ql[...])
    row = iota((2 * LANES, 2 * LANES), 0)
    col = iota((2 * LANES, 2 * LANES), 1)
    pairs = jnp.where(((row >> 3) & 15) == ((col >> 3) & 15), pairs, 0.0)
    sums = jnp.sum(pairs.reshape(2, 16, 8, 2 * LANES), axis=1)
    halves = []
    for half in range(2):
        value = sums[:, :, half * LANES : half * LANES + LANES].reshape(16, LANES)
        for shift in (64, 32, 16, 8):
            value = value + pltpu.roll(value, shift, 1)
        halves.append(value)
    both = jnp.where((lane & 8) == 0, halves[0], halves[1])
    sub = iota((8, LANES), 0)
    wide = iota((8, LANES), 1)
    for t in range(2):
        picked = jnp.where((wide >> 4) == sub, both[8 * t : 8 * t + 8], 0.0)
        zs[0, t : t + 1, :] = jnp.sum(picked, axis=0, keepdims=True)

    for phase in range(2):
        copies = []
        for k in range(1, GROUP):
            copy = pltpu.make_async_remote_copy(
                src_ref=zs.at[phase],
                dst_ref=zr.at[phase, mine[phase]],
                send_sem=ssz.at[phase, k],
                recv_sem=rsz.at[phase, mine[phase]],
                device_id=partner(phase, k),
                device_id_type=MESH,
            )
            copy.start()
            copies.append(copy)
        zr[phase, mine[phase]] = zs[phase]
        for k in range(1, GROUP):
            source = (mine[phase] + k) % GROUP
            pltpu.make_async_remote_copy(
                src_ref=zs.at[phase],
                dst_ref=zr.at[phase, source],
                send_sem=ssz.at[phase, k],
                recv_sem=rsz.at[phase, source],
                device_id=partner(phase, k),
                device_id_type=MESH,
            ).wait_recv()
        total = zr[phase, 0]
        for s in range(1, GROUP):
            total = total + zr[phase, s]
        if phase == 0:
            zs[1] = total
        else:
            gram_out[...] = total
        for copy in copies:
            copy.wait_send()

    for r, sent in enumerate(x_sends):
        for side in range(2):
            @pl.when(sent[side])
            def _():
                copy_to(r, side).wait_send()
    for r, sent in enumerate(y_sends):
        for side in range(2 if sent else 0):
            @pl.when(sent[side])
            def _():
                copy_to(r, 2 + side).wait_send()
    for side in range(2):
        @pl.when(far_side[side])
        def _():
            damping_copy(side).wait_send()

    for result in results:
        result.wait()


def finish_kernel(
    unknowns, qh_hbm, ql_hbm, gram, slots_hbm, basis_out, factor_out,
    slots, qh, ql, stage, factor, load_sem, sems, factor_sem,
):
    loads = [
        pltpu.make_async_copy(slots_hbm, slots, load_sem.at[0]),
        pltpu.make_async_copy(qh_hbm, qh, load_sem.at[1]),
        pltpu.make_async_copy(ql_hbm, ql, load_sem.at[2]),
    ]
    for load in loads:
        load.start()
    sub = iota((8, LANES), 0)
    lane = iota((8, LANES), 1)
    tiles = []
    for t in range(2):
        value = jnp.where((lane >> 4) == sub, gram[t : t + 1, :], 0.0)
        for shift in (64, 32, 16):
            value = value + pltpu.roll(value, shift, 1)
        tiles.append(value)
    low = (lane & 8) == 0
    a11 = jnp.where(low, tiles[0], pltpu.roll(tiles[0], 8, 1))
    a12 = jnp.where(low, pltpu.roll(tiles[0], LANES - 8, 1), tiles[0])
    a21 = jnp.where(low, tiles[1], pltpu.roll(tiles[1], 8, 1))
    a22 = jnp.where(low, pltpu.roll(tiles[1], LANES - 8, 1), tiles[1])
    root = math.sqrt(unknowns)
    h = step_size
    work = []
    for w in range(2):
        angle = omegas[w] * h
        work.append([
            a11 + a22 + math.cos(angle) * (a12 + a21),
            math.sin(angle) * (a21 - a12),
            jnp.where((lane & 7) == sub, 1.0, 0.0),
            jnp.zeros((8, LANES), f32),
        ])
    for i in range(8):
        below, here = sub > i, sub == i
        for w in range(2):
            g_re, g_im, m_re, m_im = work[w]
            c_re = jnp.sum(jnp.where(lane == i, g_re, 0.0), axis=1, keepdims=True)
            c_im = jnp.sum(jnp.where(lane == i, g_im, 0.0), axis=1, keepdims=True)
            pivot = c_re[i : i + 1, :]
            inverse = 1.0 / jnp.sqrt(pivot)
            c_re = c_re / pivot
            c_im = c_im / pivot

            def update(re, im):
                r_re, r_im = re[i : i + 1, :], im[i : i + 1, :]
                new_re = re - (c_re * r_re - c_im * r_im)
                new_im = im - (c_re * r_im + c_im * r_re)
                return (
                    jnp.where(below, new_re, jnp.where(here, re * inverse, re)),
                    jnp.where(below, new_im, jnp.where(here, im * inverse, im)),
                )

            g_re, g_im = update(g_re, g_im)
            m_re, m_im = update(m_re, m_im)
            work[w] = [g_re, g_im, m_re, m_im]
    for w in range(2):
        g_re, g_im = work[w][:2]
        factor[w, 0] = jnp.where(lane >= sub, g_re * (h / root), 0.0)[:, :8]
        factor[w, 1] = jnp.where(lane > sub, g_im * (h / root), 0.0)[:, :8]
    copies = [pltpu.make_async_copy(factor, factor_out, factor_sem)]
    copies[0].start()
    for load in loads:
        load.wait()
    keep = (iota((LANES, LANES), 0) & 15) == lane_slots(slots)
    q_high, q_low = qh[...], ql[...]
    for w in range(2):
        m_re, m_im = work[w][2:]
        for p in range(2):
            blocks = []
            for n in range(2):
                c, s = math.cos(omegas[w] * h * (n + 1)), math.sin(omegas[w] * h * (n + 1))
                if p == 0:
                    coef = root * (c * m_re - s * m_im)
                else:
                    coef = -root * (s * m_re + c * m_im)
                coef = jnp.broadcast_to(coef[:, None, :], (8, 16, LANES)).reshape(LANES, LANES)
                blocks.append(jnp.where(keep, coef, 0.0))
            high, low_part = split(jnp.concatenate(blocks, axis=1))
            result = mm(high, q_high) + (mm(high, q_low) + mm(low_part, q_high))
            stage[w, p] = result.reshape(8, 16, NODES)
            copy = pltpu.make_async_copy(stage.at[w, p], basis_out.at[w, p], sems.at[w, p])
            copy.start()
            copies.append(copy)
    for copy in copies:
        copy.wait()


def on_device(forcing, scale, damping, volume, lift, slots):
    hbm = pl.BlockSpec(memory_space=pltpu.HBM)
    vmem = pl.BlockSpec(memory_space=pltpu.VMEM)
    state = pltpu.VMEM((NODES, LANES), f32)
    q_high, q_low, gram = pl.pallas_call(
        march_kernel,
        out_shape=(
            jax.ShapeDtypeStruct((2 * LANES, NODES), bf16),
            jax.ShapeDtypeStruct((2 * LANES, NODES), bf16),
            jax.ShapeDtypeStruct((2, LANES), f32),
        ),
        in_specs=[hbm] * 6,
        out_specs=(hbm, hbm, vmem),
        scratch_shapes=[
            pltpu.SMEM(slots.shape, jnp.int32),
            pltpu.SMEM(scale.shape, f32),
            pltpu.VMEM(forcing.shape, bf16),
            pltpu.VMEM((NODES, NODES), f32),
            pltpu.VMEM((6 * FACE, NODES), f32),
            pltpu.VMEM((5, 2 * FACE, LANES), f32),
            pltpu.VMEM((16, NODES), f32),
            pltpu.VMEM((NODES, KDIM), bf16),
            pltpu.VMEM((NODES, KDIM), bf16),
            state, state, state, state, state, state,
            pltpu.VMEM((2 * FACE, LANES), f32),
            pltpu.VMEM((KDIM, 2 * LANES), bf16),
            state,
            pltpu.VMEM((NODES, 2 * LANES), bf16),
            pltpu.VMEM((NODES, 2 * LANES), bf16),
            pltpu.VMEM((2 * LANES, NODES), bf16),
            pltpu.VMEM((2 * LANES, NODES), bf16),
            pltpu.VMEM((3, FACE, LANES), f32),
            state,
            pltpu.VMEM((40, LANES), f32),
            pltpu.VMEM((40, LANES), f32),
            pltpu.VMEM((5, 2, FACE, LANES), f32),
            pltpu.VMEM((6, 2, 40, LANES), f32),
            pltpu.VMEM((5, 2, FACE, LANES), f32),
            pltpu.VMEM((6, 2, 40, LANES), f32),
            pltpu.VMEM((2, 2, LANES), f32),
            pltpu.VMEM((2, GROUP, 2, LANES), f32),
            pltpu.SemaphoreType.DMA((9,)),
            pltpu.SemaphoreType.DMA((5, 2)),
            pltpu.SemaphoreType.DMA((5, 2)),
            pltpu.SemaphoreType.DMA((6, 2)),
            pltpu.SemaphoreType.DMA((6, 2)),
            pltpu.SemaphoreType.DMA((1,)),
            pltpu.SemaphoreType.DMA((1,)),
            pltpu.SemaphoreType.DMA((2, GROUP)),
            pltpu.SemaphoreType.DMA((2, GROUP)),
            pltpu.SemaphoreType.DMA((2,)),
        ],
        compiler_params=pltpu.CompilerParams(
            collective_id=0, has_side_effects=True, vmem_limit_bytes=64 * 1024 * 1024
        ),
        name="march",
    )(forcing, scale, damping, volume, lift, slots)
    unknowns = forcing.shape[3] * NODES * lax.axis_size("gx") * lax.axis_size("gy")
    shape = forcing.shape
    return pl.pallas_call(
        lambda *refs: finish_kernel(unknowns, *refs),
        out_shape=(
            jax.ShapeDtypeStruct(shape, f32),
            jax.ShapeDtypeStruct((2, 2, 8, 8), f32),
        ),
        in_specs=[hbm, hbm, vmem, hbm],
        out_specs=(hbm, hbm),
        scratch_shapes=[
            pltpu.SMEM(slots.shape, jnp.int32),
            pltpu.VMEM((2 * LANES, NODES), bf16),
            pltpu.VMEM((2 * LANES, NODES), bf16),
            pltpu.VMEM(shape, f32),
            pltpu.VMEM((2, 2, 8, 8), f32),
            pltpu.SemaphoreType.DMA((3,)),
            pltpu.SemaphoreType.DMA((2, 2)),
            pltpu.SemaphoreType.DMA,
        ],
        compiler_params=pltpu.CompilerParams(vmem_limit_bytes=64 * 1024 * 1024),
        name="finish",
    )(q_high, q_low, gram, slots)


def solution(mesh):
    placed = (
        P(None, None, None, ("gx", "gy"), None),
        P(("gx", "gy")),
        P(("gx", "gy"), None),
        P(),
        P(),
        P("gx", "gy", None),
    )
    return jax.shard_map(
        on_device,
        mesh=mesh,
        in_specs=placed,
        out_specs=(P(None, None, None, ("gx", "gy"), None), P()),
        check_vma=False,
    )
```

```python
import math

import jax
import jax.numpy as jnp
from jax import lax
from jax.experimental import pallas as pl
from jax.experimental.pallas import tpu as pltpu
from jax.sharding import PartitionSpec as P

NODES = 640
FACE = 160
LANES = 128
KDIM = NODES + 6 * FACE
step_size = 0.4
omegas = (1.3, 3.1)
MESH = pl.DeviceIdType.MESH
f32 = jnp.float32
bf16 = jnp.bfloat16
GROUP = 16
FAR_FIRST = (
    (8, 7, 9, 6, 10, 5, 11, 4, 12, 3, 13, 2, 14, 1, 15),
    (10, 6, 9, 11, 7, 5, 8, 2, 14, 13, 3, 12, 4, 1, 15),
)


def iota(shape, dim):
    return lax.broadcasted_iota(jnp.int32, shape, dim)


def split(value):
    high = value.astype(bf16)
    return high, (value - high.astype(f32)).astype(bf16)


def mm(left, right):
    return lax.dot_general(left, right, (((1,), (0,)), ((), ())), preferred_element_type=f32)


def lane_slots(slots_ref):
    group = iota((1, LANES), 1) >> 3
    result = jnp.zeros((1, LANES), jnp.int32)
    for g in range(16):
        result = jnp.where(group == g, slots_ref[0, g // 4, g % 4], result)
    return result


def placement(slots_ref):
    row = iota((LANES, LANES), 0)
    lane = iota((LANES, LANES), 1)
    return ((row >> 4) == (lane & 7)) & ((row & 15) == lane_slots(slots_ref))


def march_kernel(
    forcing, scale_hbm, damping, volume, lift, slots_hbm,
    qh_out, ql_out, gram_out,
    slots, scale, fb, vol, lft, lfy, dmp, wh, wl, f1, f2, st, q1, k1, dt, jump, xb, acc,
    qh, ql, th, tl, corr, gst, sd, rd,
    sx, sy, rx, ry, zs, zr,
    load_sem, ssx, rsx, ssy, rsy, ssd, rsd, ssz, rsz, out_sem,
):
    gx, gy = lax.axis_index("gx"), lax.axis_index("gy")
    last_x, last_y = lax.axis_size("gx") - 1, lax.axis_size("gy") - 1
    h = step_size

    pairs = [
        (slots_hbm, slots),
        (forcing.at[0, 0], fb.at[0, 0]),
        (forcing.at[1, 0], fb.at[1, 0]),
        (scale_hbm, scale),
        (volume, vol),
        (lift, lft),
        (damping, dmp),
        (forcing.at[0, 1], fb.at[0, 1]),
        (forcing.at[1, 1], fb.at[1, 1]),
    ]
    loads = [
        pltpu.make_async_copy(source, target, load_sem.at[n])
        for n, (source, target) in enumerate(pairs)
    ]

    sides = [
        (gx > 0, (gx - 1, gy)),
        (gx < last_x, (gx + 1, gy)),
        (gy > 0, (gx, gy - 1)),
        (gy < last_y, (gx, gy + 1)),
    ]
    yy, zh, xx = gx // 8, (gx // 4) % 2, gx % 4
    mine = [zh * 8 + gy, yy * 4 + xx]

    def partner(phase, k):
        p = (mine[phase] + k) % GROUP
        if phase == 0:
            return (yy * 8 + (p // 8) * 4 + xx, p % 8)
        return ((p // 4) * 8 + zh * 4 + p % 4, gy)

    far_side = [
        jnp.logical_and(gx > 0, xx == 0),
        jnp.logical_and(gx < last_x, xx == 3),
    ]

    far_any = jnp.logical_or(far_side[0], far_side[1])
    near_side = [
        jnp.logical_and(sides[n][0], jnp.logical_not(far_side[n])) for n in range(2)
    ]
    far_y = [jnp.logical_and(sides[2 + n][0], far_any) for n in range(2)]
    all_x, all_y = [sides[0][0], sides[1][0]], [sides[2][0], sides[3][0]]
    x_sends = [all_x, far_side, near_side, far_side, near_side]
    y_sends = [all_y, far_y, all_y, [], all_y, far_y]

    barrier = pltpu.get_barrier_semaphore()
    expected = 2 * (GROUP - 1)
    for there, place in sides:
        expected = expected + there.astype(jnp.int32)

        @pl.when(there)
        def _():
            pl.semaphore_signal(barrier, inc=1, device_id=place, device_id_type=MESH)

    for load in loads:
        load.start()
    for phase in range(2):
        for k in FAR_FIRST[phase]:
            pl.semaphore_signal(
                barrier, inc=1, device_id=partner(phase, k), device_id_type=MESH
            )

    for side in range(4):
        land = rx if side < 2 else ry

        @pl.when(jnp.logical_not(sides[side][0]))
        def _():
            for r in range(land.shape[0]):
                land[r, side % 2] = jnp.zeros(land.shape[2:], f32)

    loads[0].wait()
    one_hot = placement(slots).astype(f32).astype(bf16)
    slot_of = lane_slots(slots)

    def part(w, p):
        rows = fb[w, p].reshape(LANES, NODES)
        return lax.dot_general(rows, one_hot, (((0,), (0,)), ((), ())), preferred_element_type=f32)

    loads[1].wait()
    loads[2].wait()
    f00, f10 = part(0, 0), part(1, 0)
    k1[...] = f00 + f10
    st[...] = h * k1[...]

    lane = iota((1, LANES), 1)
    quarter = lane >> 5
    span = (lane >> 3) & 3

    def copy_to(r, side):
        out, land = (sx, rx) if side < 2 else (sy, ry)
        s_sem, r_sem = (ssx, rsx) if side < 2 else (ssy, rsy)
        return pltpu.make_async_remote_copy(
            src_ref=out.at[r, side % 2],
            dst_ref=land.at[r, 1 - side % 2],
            send_sem=s_sem.at[r, side % 2],
            recv_sem=r_sem.at[r, 1 - side % 2],
            device_id=sides[side][1],
            device_id_type=MESH,
        )

    def arrival(r, side):
        out, land = (sx, rx) if side < 2 else (sy, ry)
        s_sem, r_sem = (ssx, rsx) if side < 2 else (ssy, rsy)
        return pltpu.make_async_remote_copy(
            src_ref=out.at[r, side % 2],
            dst_ref=land.at[r, side % 2],
            send_sem=s_sem.at[r, side % 2],
            recv_sem=r_sem.at[r, side % 2],
            device_id=sides[side][1],
            device_id_type=MESH,
        )

    def y_block(src, e, high):
        return src[pl.ds((12 if high else 0) + e, 40, stride=16), :]

    def face(src, side):
        start = 48 if side else 0
        return src[...].reshape(10, 64, LANES)[:, start : start + 16].reshape(FACE, LANES)

    def send_x(r, side, src, when=None):
        @pl.when(x_sends[r][side] if when is None else when)
        def _():
            sx[r, side] = face(src, side)
            copy_to(r, side).start()

    def send_y(r, src):
        for high in range(2):
            packed = jnp.zeros((40, LANES), f32)
            for e in range(4):
                shift = (32 * e - (96 if high else 0)) % LANES
                block = y_block(src, e, high)
                if shift:
                    block = pltpu.roll(block, shift, 1)
                packed = jnp.where(quarter == e, block, packed)

            @pl.when(y_sends[r][high])
            def _():
                sy[r, high] = packed
                copy_to(r, 2 + high).start()

    def to_operand(row, value):
        high, low = split(value)
        rows = pl.ds(row, value.shape[0])
        xb[rows, 0:LANES] = high
        xb[rows, LANES:] = low

    def products(ranges, done):
        for block in range(5):
            rows = slice(block * 128, block * 128 + 128)
            both = None
            for lo, hi in ranges:
                wide = mm(wh[rows, lo:hi], xb[lo:hi, :])
                term = wide[:, :LANES] + wide[:, LANES:] + mm(wl[rows, lo:hi], xb[lo:hi, :LANES])
                both = term if both is None else both + term
            done(rows, both)

    def begin(rows, value):
        acc[rows, :] = value

    def add(rows, value):
        acc[rows, :] = acc[rows, :] + value

    def far_value(rows, value):
        st[rows, :] = st[rows, :] + 0.5 * h * value

    def ghost_value(rows, value):
        gst[rows, :] = 0.5 * h * value

    X_ROWS = [(NODES, NODES + 2 * FACE)]
    OWN_ROWS = [(0, NODES), (NODES + 4 * FACE, KDIM)]
    FACE_ROWS = [(NODES, NODES + 4 * FACE)]

    def face_products(side, ranges):
        start = 48 if side else 0
        rows = [slice(64 * f + start, 64 * f + start + 16) for f in range(10)]
        total = None
        for lo, hi in ranges:
            left_high = jnp.concatenate([wh[r, lo:hi] for r in rows], axis=0)
            left_low = jnp.concatenate([wl[r, lo:hi] for r in rows], axis=0)
            wide = mm(left_high, xb[lo:hi, :])
            value = wide[:, :LANES] + wide[:, LANES:] + mm(left_low, xb[lo:hi, :LANES])
            total = value if total is None else total + value
        return total

    def set_x(side, value):
        to_operand(NODES + side * FACE, value)

    def span_jumps(src):
        low = src[pl.ds(0, FACE, stride=4), :]
        high = src[pl.ds(3, FACE, stride=4), :]
        near = jnp.where(span == 0, pltpu.roll(high, LANES - 24, 1), pltpu.roll(high, 8, 1))
        to_operand(NODES + 4 * FACE, near - low)
        near = jnp.where(span == 3, pltpu.roll(low, 24, 1), pltpu.roll(low, LANES - 8, 1))
        to_operand(NODES + 5 * FACE, near - high)

    def y_jumps(src, r):
        for side in (2, 3):
            @pl.when(y_sends[r][side - 2])
            def _():
                arrival(r, side).wait_recv()
        for e in range(4):
            rows = slice(40 * e, 40 * e + 40)
            low, high = y_block(src, e, 0), y_block(src, e, 1)
            far = ry[r, 0]
            if e:
                far = pltpu.roll(far, LANES - 32 * e, 1)
            jump[rows, :] = jnp.where(quarter == 0, far, pltpu.roll(high, 32, 1)) - low
            far = ry[r, 1]
            if e < 3:
                far = pltpu.roll(far, 96 - 32 * e, 1)
            rows = slice(FACE + 40 * e, FACE + 40 * e + 40)
            jump[rows, :] = jnp.where(quarter == 3, far, pltpu.roll(low, LANES - 32, 1)) - high
        to_operand(NODES + 2 * FACE, jump[...])

    def operate_own(src):
        to_operand(0, scale_lane * src[...])
        span_jumps(src)
        products(OWN_ROWS, begin)

    def operate_rest(src):
        products(FACE_ROWS, add)
        acc[...] = acc[...] - dt[...] * src[...]

    loads[3].wait()
    scale_lane = jnp.zeros((1, LANES), f32)
    for s in range(16):
        scale_lane = jnp.where(slot_of == s, scale[s], scale_lane)

    def turn(source, column):
        high, low = split(source.T)
        wh[:, column : column + source.shape[0]] = high
        wl[:, column : column + source.shape[0]] = low

    loads[4].wait()
    for block in range(5):
        turn(vol[block * 128 : block * 128 + 128, :], block * 128)
    loads[5].wait()
    for b in range(5):
        columns = slice(b * 128, b * 128 + 128)
        lfy[b] = lft[2 * FACE : 4 * FACE, columns]
        for high in range(2):
            for e in range(4):
                row = 2 * FACE + high * FACE + 40 * e
                lft[row : row + 40, columns] = lfy[b, pl.ds(high * FACE + e, 40, stride=4), :]
    for block in range(7):
        turn(lft[block * 128 : block * 128 + 128, :], NODES + block * 128)
    turn(lft[896:960, :], NODES + 896)

    loads[6].wait()
    spread16 = jnp.where(iota((16, LANES), 0) == slot_of, 1.0, 0.0).astype(bf16)
    rest = dmp[...]
    total = jnp.zeros((NODES, LANES), f32)
    for _ in range(3):
        piece = rest.astype(bf16)
        rest = rest - piece.astype(f32)
        total = total + lax.dot_general(
            piece, spread16, (((0,), (0,)), ((), ())), preferred_element_type=f32
        )
    dt[...] = total

    loads[7].wait()
    loads[8].wait()
    f00, f01, f10, f11 = part(0, 0), part(0, 1), part(1, 0), part(1, 1)

    def forcing_at(moment):
        a, b = omegas[0] * moment, omegas[1] * moment
        return (
            f00 * math.cos(a) - f01 * math.sin(a) + f10 * math.cos(b) - f11 * math.sin(b)
        )

    f1[...] = forcing_at(h)
    f2[...] = forcing_at(2 * h)

    operate_own(st)
    pl.semaphore_wait(barrier, expected)
    for side in range(2):
        send_x(0, side, st, near_side[side])
    send_y(0, st)
    for side in range(2):
        send_x(0, side, st, far_side[side])
    y_jumps(st, 0)
    for side in range(2):
        @pl.when(near_side[side])
        def _():
            arrival(0, side).wait_recv()

        @pl.when(far_side[side])
        def _():
            set_x(side, -face(st, side))

        @pl.when(jnp.logical_not(far_side[side]))
        def _():
            set_x(side, rx[0, side] - face(st, side))

    operate_rest(st)
    st[...] = 0.5 * h * (k1[...] + acc[...] + f1[...])


    def damping_copy(side):
        return pltpu.make_async_remote_copy(
            src_ref=sd, dst_ref=rd, send_sem=ssd.at[0], recv_sem=rsd.at[0],
            device_id=sides[side][1], device_id_type=MESH,
        )

    @pl.when(far_any)
    def _():
        send_y(1, st)
        for side in range(2):
            send_x(1, side, st)
        to_operand(0, scale_lane * st[...])
        span_jumps(st)
        for side in range(2):
            @pl.when(far_side[side])
            def _():
                set_x(side, -face(st, side))
                corr[1] = face_products(side, OWN_ROWS)

        y_jumps(st, 1)
        for side in range(2):
            @pl.when(far_side[side])
            def _():
                arrival(2, 1 - side).wait_recv()
                set_x(1 - side, rx[2, 1 - side] - face(st, 1 - side))
                slope = corr[1] + face_products(side, FACE_ROWS)
                slope = slope - face(dt, side) * face(st, side) + face(f1, side)
                sx[3, side] = face(st, side) + h * slope

        for side in range(2):
            @pl.when(far_side[side])
            def _():
                set_x(side, jnp.zeros((FACE, LANES), f32))
                set_x(1 - side, sx[0, side])
                mine_damped = face(dt, side)
                packed = [jnp.zeros((16, LANES), f32), jnp.zeros((16, LANES), f32)]
                for b in range(10):
                    piece = mine_damped[16 * b : 16 * b + 16]
                    packed[b // 8] = jnp.where((lane & 7) == b % 8, piece, packed[b // 8])
                sd[0:16, :] = packed[0]
                sd[16:32, :] = packed[1]
                sd[32:, :] = jnp.broadcast_to(scale_lane, (8, LANES))

        products(X_ROWS, ghost_value)
        send_y(5, gst)
        for side in range(2):
            @pl.when(far_side[side])
            def _():
                arrival(0, side).wait_recv()
                set_x(side, rx[0, side])
                set_x(1 - side, jnp.zeros((FACE, LANES), f32))
                inner = face_products(1 - side, X_ROWS)
                sx[2, 1 - side] = face(st, 1 - side) + 0.5 * h * inner
                copy_to(2, 1 - side).start()

        products(X_ROWS, far_value)

    send_y(2, st)
    for side in range(2):
        send_x(2, side, st, jnp.logical_and(near_side[side], jnp.logical_not(far_any)))
    for side in range(2):
        @pl.when(far_side[side])
        def _():
            copy_to(3, side).start()
            damping_copy(side).start()

    q1[...] = st[...]

    def keep_state(n, value):
        lanes = slice(n * LANES, n * LANES + LANES)
        high, low = split(value)
        qh[:, lanes] = high
        ql[:, lanes] = low
        high, low = split(value.T)
        th[lanes, :] = high
        tl[lanes, :] = low

    @pl.when(far_any)
    def _():
        to_operand(0, gst[...])
        span_jumps(gst)
        y_jumps(gst, 5)
        for side in range(2):
            set_x(side, -face(gst, side))
        for side in range(2):
            @pl.when(far_side[side])
            def _():
                other = 1 - side
                corr[0] = face(gst, other)
                corr[1] = face_products(other, [(0, NODES)])
                corr[2] = face_products(other, [(NODES, KDIM)])

    operate_own(st)
    y_jumps(st, 2)
    for side in range(2):
        @pl.when(jnp.logical_and(near_side[side], jnp.logical_not(far_any)))
        def _():
            arrival(2, side).wait_recv()

        @pl.when(far_side[side])
        def _():
            arrival(1, side).wait_recv()
            set_x(side, rx[1, side] + corr[0] - face(st, side))

        @pl.when(jnp.logical_not(far_side[side]))
        def _():
            set_x(side, rx[2, side] - face(st, side))

    for side in range(2):
        @pl.when(near_side[side])
        def _():
            slope = face(acc, side) + face_products(side, FACE_ROWS)
            slope = slope - face(dt, side) * face(st, side) + face(f1, side)
            sx[4, side] = face(q1, side) + h * slope
            copy_to(4, side).start()

    operate_rest(st)
    k1[...] = acc[...] + f1[...]
    st[...] = q1[...] + h * k1[...]
    send_y(4, st)
    operate_own(st)
    keep_state(0, q1[...])

    for side in range(2):
        @pl.when(far_side[side])
        def _():
            other = 1 - side
            set_x(side, jnp.zeros((FACE, LANES), f32))
            set_x(other, face(q1, side))
            direct = face_products(other, X_ROWS)
            damping_copy(side).wait_recv()
            damped = []
            for b in range(10):
                piece = rd[16 * (b // 8) : 16 * (b // 8) + 16, :]
                piece = jnp.where((lane & 7) == b % 8, piece, 0.0)
                if b % 8:
                    piece = pltpu.roll(piece, LANES - b % 8, 1)
                for shift in (1, 2, 4):
                    piece = piece + pltpu.roll(piece, shift, 1)
                damped.append(piece)
            damped = jnp.concatenate(damped, axis=0)
            change = rd[32:33, :] * corr[1] + corr[2] - damped * corr[0] + direct
            corr[0] = corr[0] + h * change

    y_jumps(st, 4)
    for side in range(2):
        @pl.when(near_side[side])
        def _():
            arrival(4, side).wait_recv()

        @pl.when(far_side[side])
        def _():
            arrival(3, side).wait_recv()
            set_x(side, rx[3, side] + corr[0] - face(st, side))

        @pl.when(jnp.logical_not(far_side[side]))
        def _():
            set_x(side, rx[4, side] - face(st, side))

    operate_rest(st)
    keep_state(1, q1[...] + 0.5 * h * (k1[...] + acc[...] + f2[...]))
    results = [
        pltpu.make_async_copy(th, qh_out, out_sem.at[0]),
        pltpu.make_async_copy(tl, ql_out, out_sem.at[1]),
    ]
    for result in results:
        result.start()

    pairs = mm(th[...], qh[...]) + (mm(th[...], ql[...]) + mm(tl[...], qh[...])) + mm(tl[...], ql[...])
    row = iota((2 * LANES, 2 * LANES), 0)
    col = iota((2 * LANES, 2 * LANES), 1)
    pairs = jnp.where(((row >> 3) & 15) == ((col >> 3) & 15), pairs, 0.0)
    sums = jnp.sum(pairs.reshape(2, 16, 8, 2 * LANES), axis=1)
    halves = []
    for half in range(2):
        value = sums[:, :, half * LANES : half * LANES + LANES].reshape(16, LANES)
        for shift in (64, 32, 16, 8):
            value = value + pltpu.roll(value, shift, 1)
        halves.append(value)
    both = jnp.where((lane & 8) == 0, halves[0], halves[1])
    sub = iota((8, LANES), 0)
    wide = iota((8, LANES), 1)
    for t in range(2):
        picked = jnp.where((wide >> 4) == sub, both[8 * t : 8 * t + 8], 0.0)
        zs[0, t : t + 1, :] = jnp.sum(picked, axis=0, keepdims=True)

    copies = []
    for phase in range(2):
        for k in FAR_FIRST[phase]:
            copy = pltpu.make_async_remote_copy(
                src_ref=zs.at[phase],
                dst_ref=zr.at[phase, mine[phase]],
                send_sem=ssz.at[phase, k],
                recv_sem=rsz.at[phase, mine[phase]],
                device_id=partner(phase, k),
                device_id_type=MESH,
            )
            copy.start()
            copies.append(copy)
        zr[phase, mine[phase]] = zs[phase]
        for k in range(1, GROUP):
            source = (mine[phase] + k) % GROUP
            pltpu.make_async_remote_copy(
                src_ref=zs.at[phase],
                dst_ref=zr.at[phase, source],
                send_sem=ssz.at[phase, k],
                recv_sem=rsz.at[phase, source],
                device_id=partner(phase, k),
                device_id_type=MESH,
            ).wait_recv()
        total = zr[phase, 0]
        for s in range(1, GROUP):
            total = total + zr[phase, s]
        if phase == 0:
            zs[1] = total
        else:
            gram_out[...] = total
    for copy in copies:
        copy.wait_send()

    for r, sent in enumerate(x_sends):
        for side in range(2):
            @pl.when(sent[side])
            def _():
                copy_to(r, side).wait_send()
    for r, sent in enumerate(y_sends):
        for side in range(2 if sent else 0):
            @pl.when(sent[side])
            def _():
                copy_to(r, 2 + side).wait_send()
    for side in range(2):
        @pl.when(far_side[side])
        def _():
            damping_copy(side).wait_send()

    for result in results:
        result.wait()


def finish_kernel(
    unknowns, qh_hbm, ql_hbm, gram, slots_hbm, basis_out, factor_out,
    slots, qh, ql, stage, factor, load_sem, sems, factor_sem,
):
    loads = [
        pltpu.make_async_copy(slots_hbm, slots, load_sem.at[0]),
        pltpu.make_async_copy(qh_hbm, qh, load_sem.at[1]),
        pltpu.make_async_copy(ql_hbm, ql, load_sem.at[2]),
    ]
    for load in loads:
        load.start()
    sub = iota((8, LANES), 0)
    lane = iota((8, LANES), 1)
    tiles = []
    for t in range(2):
        value = jnp.where((lane >> 4) == sub, gram[t : t + 1, :], 0.0)
        for shift in (64, 32, 16):
            value = value + pltpu.roll(value, shift, 1)
        tiles.append(value)
    low = (lane & 8) == 0
    a11 = jnp.where(low, tiles[0], pltpu.roll(tiles[0], 8, 1))
    a12 = jnp.where(low, pltpu.roll(tiles[0], LANES - 8, 1), tiles[0])
    a21 = jnp.where(low, tiles[1], pltpu.roll(tiles[1], 8, 1))
    a22 = jnp.where(low, pltpu.roll(tiles[1], LANES - 8, 1), tiles[1])
    root = math.sqrt(unknowns)
    h = step_size
    work = []
    for w in range(2):
        angle = omegas[w] * h
        work.append([
            a11 + a22 + math.cos(angle) * (a12 + a21),
            math.sin(angle) * (a21 - a12),
            jnp.where((lane & 7) == sub, 1.0, 0.0),
            jnp.zeros((8, LANES), f32),
        ])
    for i in range(8):
        below, here = sub > i, sub == i
        for w in range(2):
            g_re, g_im, m_re, m_im = work[w]
            c_re = jnp.sum(jnp.where(lane == i, g_re, 0.0), axis=1, keepdims=True)
            c_im = jnp.sum(jnp.where(lane == i, g_im, 0.0), axis=1, keepdims=True)
            pivot = c_re[i : i + 1, :]
            inverse = 1.0 / jnp.sqrt(pivot)
            c_re = c_re / pivot
            c_im = c_im / pivot

            def update(re, im):
                r_re, r_im = re[i : i + 1, :], im[i : i + 1, :]
                new_re = re - (c_re * r_re - c_im * r_im)
                new_im = im - (c_re * r_im + c_im * r_re)
                return (
                    jnp.where(below, new_re, jnp.where(here, re * inverse, re)),
                    jnp.where(below, new_im, jnp.where(here, im * inverse, im)),
                )

            g_re, g_im = update(g_re, g_im)
            m_re, m_im = update(m_re, m_im)
            work[w] = [g_re, g_im, m_re, m_im]
    for w in range(2):
        g_re, g_im = work[w][:2]
        factor[w, 0] = jnp.where(lane >= sub, g_re * (h / root), 0.0)[:, :8]
        factor[w, 1] = jnp.where(lane > sub, g_im * (h / root), 0.0)[:, :8]
    copies = [pltpu.make_async_copy(factor, factor_out, factor_sem)]
    copies[0].start()
    for load in loads:
        load.wait()
    keep = (iota((LANES, LANES), 0) & 15) == lane_slots(slots)
    q_high, q_low = qh[...], ql[...]
    for w in range(2):
        m_re, m_im = work[w][2:]
        for p in range(2):
            blocks = []
            for n in range(2):
                c, s = math.cos(omegas[w] * h * (n + 1)), math.sin(omegas[w] * h * (n + 1))
                if p == 0:
                    coef = root * (c * m_re - s * m_im)
                else:
                    coef = -root * (s * m_re + c * m_im)
                coef = jnp.broadcast_to(coef[:, None, :], (8, 16, LANES)).reshape(LANES, LANES)
                blocks.append(jnp.where(keep, coef, 0.0))
            high, low_part = split(jnp.concatenate(blocks, axis=1))
            result = mm(high, q_high) + (mm(high, q_low) + mm(low_part, q_high))
            stage[w, p] = result.reshape(8, 16, NODES)
            copy = pltpu.make_async_copy(stage.at[w, p], basis_out.at[w, p], sems.at[w, p])
            copy.start()
            copies.append(copy)
    for copy in copies:
        copy.wait()


def on_device(forcing, scale, damping, volume, lift, slots):
    hbm = pl.BlockSpec(memory_space=pltpu.HBM)
    vmem = pl.BlockSpec(memory_space=pltpu.VMEM)
    state = pltpu.VMEM((NODES, LANES), f32)
    q_high, q_low, gram = pl.pallas_call(
        march_kernel,
        out_shape=(
            jax.ShapeDtypeStruct((2 * LANES, NODES), bf16),
            jax.ShapeDtypeStruct((2 * LANES, NODES), bf16),
            jax.ShapeDtypeStruct((2, LANES), f32),
        ),
        in_specs=[hbm] * 6,
        out_specs=(hbm, hbm, vmem),
        scratch_shapes=[
            pltpu.SMEM(slots.shape, jnp.int32),
            pltpu.SMEM(scale.shape, f32),
            pltpu.VMEM(forcing.shape, bf16),
            pltpu.VMEM((NODES, NODES), f32),
            pltpu.VMEM((6 * FACE, NODES), f32),
            pltpu.VMEM((5, 2 * FACE, LANES), f32),
            pltpu.VMEM((16, NODES), f32),
            pltpu.VMEM((NODES, KDIM), bf16),
            pltpu.VMEM((NODES, KDIM), bf16),
            state, state, state, state, state, state,
            pltpu.VMEM((2 * FACE, LANES), f32),
            pltpu.VMEM((KDIM, 2 * LANES), bf16),
            state,
            pltpu.VMEM((NODES, 2 * LANES), bf16),
            pltpu.VMEM((NODES, 2 * LANES), bf16),
            pltpu.VMEM((2 * LANES, NODES), bf16),
            pltpu.VMEM((2 * LANES, NODES), bf16),
            pltpu.VMEM((3, FACE, LANES), f32),
            state,
            pltpu.VMEM((40, LANES), f32),
            pltpu.VMEM((40, LANES), f32),
            pltpu.VMEM((5, 2, FACE, LANES), f32),
            pltpu.VMEM((6, 2, 40, LANES), f32),
            pltpu.VMEM((5, 2, FACE, LANES), f32),
            pltpu.VMEM((6, 2, 40, LANES), f32),
            pltpu.VMEM((2, 2, LANES), f32),
            pltpu.VMEM((2, GROUP, 2, LANES), f32),
            pltpu.SemaphoreType.DMA((9,)),
            pltpu.SemaphoreType.DMA((5, 2)),
            pltpu.SemaphoreType.DMA((5, 2)),
            pltpu.SemaphoreType.DMA((6, 2)),
            pltpu.SemaphoreType.DMA((6, 2)),
            pltpu.SemaphoreType.DMA((1,)),
            pltpu.SemaphoreType.DMA((1,)),
            pltpu.SemaphoreType.DMA((2, GROUP)),
            pltpu.SemaphoreType.DMA((2, GROUP)),
            pltpu.SemaphoreType.DMA((2,)),
        ],
        compiler_params=pltpu.CompilerParams(
            collective_id=0, has_side_effects=True, vmem_limit_bytes=64 * 1024 * 1024
        ),
        name="march",
    )(forcing, scale, damping, volume, lift, slots)
    unknowns = forcing.shape[3] * NODES * lax.axis_size("gx") * lax.axis_size("gy")
    shape = forcing.shape
    return pl.pallas_call(
        lambda *refs: finish_kernel(unknowns, *refs),
        out_shape=(
            jax.ShapeDtypeStruct(shape, f32),
            jax.ShapeDtypeStruct((2, 2, 8, 8), f32),
        ),
        in_specs=[hbm, hbm, vmem, hbm],
        out_specs=(hbm, hbm),
        scratch_shapes=[
            pltpu.SMEM(slots.shape, jnp.int32),
            pltpu.VMEM((2 * LANES, NODES), bf16),
            pltpu.VMEM((2 * LANES, NODES), bf16),
            pltpu.VMEM(shape, f32),
            pltpu.VMEM((2, 2, 8, 8), f32),
            pltpu.SemaphoreType.DMA((3,)),
            pltpu.SemaphoreType.DMA((2, 2)),
            pltpu.SemaphoreType.DMA,
        ],
        compiler_params=pltpu.CompilerParams(vmem_limit_bytes=64 * 1024 * 1024),
        name="finish",
    )(q_high, q_low, gram, slots)


def solution(mesh):
    placed = (
        P(None, None, None, ("gx", "gy"), None),
        P(("gx", "gy")),
        P(("gx", "gy"), None),
        P(),
        P(),
        P("gx", "gy", None),
    )
    return jax.shard_map(
        on_device,
        mesh=mesh,
        in_specs=placed,
        out_specs=(P(None, None, None, ("gx", "gy"), None), P()),
        check_vma=False,
    )
```

```python
import math

import jax
import jax.numpy as jnp
from jax import lax
from jax.experimental import pallas as pl
from jax.experimental.pallas import tpu as pltpu
from jax.sharding import PartitionSpec as P

NODES = 640
FACE = 160
LANES = 128
KDIM = NODES + 6 * FACE
step_size = 0.4
omegas = (1.3, 3.1)
MESH = pl.DeviceIdType.MESH
f32 = jnp.float32
bf16 = jnp.bfloat16
GROUP = 16


def iota(shape, dim):
    return lax.broadcasted_iota(jnp.int32, shape, dim)


def split(value):
    high = value.astype(bf16)
    return high, (value - high.astype(f32)).astype(bf16)


def mm(left, right):
    return lax.dot_general(left, right, (((1,), (0,)), ((), ())), preferred_element_type=f32)


def lane_slots(slots_ref):
    group = iota((1, LANES), 1) >> 3
    result = jnp.zeros((1, LANES), jnp.int32)
    for g in range(16):
        result = jnp.where(group == g, slots_ref[0, g // 4, g % 4], result)
    return result


def placement(slots_ref):
    row = iota((LANES, LANES), 0)
    lane = iota((LANES, LANES), 1)
    return ((row >> 4) == (lane & 7)) & ((row & 15) == lane_slots(slots_ref))


def march_kernel(
    forcing, scale_hbm, damping, volume, lift, slots_hbm,
    qh_out, ql_out, gram_out,
    slots, scale, fb, vol, lft, lfy, dmp, wh, wl, f1, f2, st, q1, k1, dt, jump, xb, acc,
    qh, ql, th, tl, corr, gst, sd, rd,
    sx, sy, rx, ry, zs, zr,
    load_sem, ssx, rsx, ssy, rsy, ssd, rsd, ssz, rsz, out_sem,
):
    gx, gy = lax.axis_index("gx"), lax.axis_index("gy")
    last_x, last_y = lax.axis_size("gx") - 1, lax.axis_size("gy") - 1
    h = step_size

    pairs = [
        (slots_hbm, slots),
        (forcing.at[0, 0], fb.at[0, 0]),
        (forcing.at[1, 0], fb.at[1, 0]),
        (scale_hbm, scale),
        (volume, vol),
        (lift, lft),
        (damping, dmp),
        (forcing.at[0, 1], fb.at[0, 1]),
        (forcing.at[1, 1], fb.at[1, 1]),
    ]
    loads = [
        pltpu.make_async_copy(source, target, load_sem.at[n])
        for n, (source, target) in enumerate(pairs)
    ]

    sides = [
        (gx > 0, (gx - 1, gy)),
        (gx < last_x, (gx + 1, gy)),
        (gy > 0, (gx, gy - 1)),
        (gy < last_y, (gx, gy + 1)),
    ]
    yy, zh, xx = gx // 8, (gx // 4) % 2, gx % 4
    mine = [zh * 8 + gy, yy * 4 + xx]

    def partner(phase, k):
        p = (mine[phase] + k) % GROUP
        if phase == 0:
            return (yy * 8 + (p // 8) * 4 + xx, p % 8)
        return ((p // 4) * 8 + zh * 4 + p % 4, gy)

    far_side = [
        jnp.logical_and(gx > 0, xx == 0),
        jnp.logical_and(gx < last_x, xx == 3),
    ]

    far_any = jnp.logical_or(far_side[0], far_side[1])
    near_side = [
        jnp.logical_and(sides[n][0], jnp.logical_not(far_side[n])) for n in range(2)
    ]
    far_y = [jnp.logical_and(sides[2 + n][0], far_any) for n in range(2)]
    all_x, all_y = [sides[0][0], sides[1][0]], [sides[2][0], sides[3][0]]
    x_sends = [all_x, far_side, near_side, far_side, near_side]
    y_sends = [all_y, far_y, all_y, [], all_y, far_y]

    barrier = pltpu.get_barrier_semaphore()
    expected = 2 * (GROUP - 1)
    for there, place in sides:
        expected = expected + there.astype(jnp.int32)

        @pl.when(there)
        def _():
            pl.semaphore_signal(barrier, inc=1, device_id=place, device_id_type=MESH)

    for load in loads:
        load.start()
    for phase in range(2):
        for k in range(1, GROUP):
            pl.semaphore_signal(
                barrier, inc=1, device_id=partner(phase, k), device_id_type=MESH
            )

    for side in range(4):
        land = rx if side < 2 else ry

        @pl.when(jnp.logical_not(sides[side][0]))
        def _():
            for r in range(land.shape[0]):
                land[r, side % 2] = jnp.zeros(land.shape[2:], f32)

    loads[0].wait()
    one_hot = placement(slots).astype(f32).astype(bf16)
    slot_of = lane_slots(slots)

    def part(w, p):
        rows = fb[w, p].reshape(LANES, NODES)
        return lax.dot_general(rows, one_hot, (((0,), (0,)), ((), ())), preferred_element_type=f32)

    loads[1].wait()
    loads[2].wait()
    f00, f10 = part(0, 0), part(1, 0)
    k1[...] = f00 + f10
    st[...] = h * k1[...]

    lane = iota((1, LANES), 1)
    quarter = lane >> 5
    span = (lane >> 3) & 3

    def copy_to(r, side):
        out, land = (sx, rx) if side < 2 else (sy, ry)
        s_sem, r_sem = (ssx, rsx) if side < 2 else (ssy, rsy)
        return pltpu.make_async_remote_copy(
            src_ref=out.at[r, side % 2],
            dst_ref=land.at[r, 1 - side % 2],
            send_sem=s_sem.at[r, side % 2],
            recv_sem=r_sem.at[r, 1 - side % 2],
            device_id=sides[side][1],
            device_id_type=MESH,
        )

    def arrival(r, side):
        out, land = (sx, rx) if side < 2 else (sy, ry)
        s_sem, r_sem = (ssx, rsx) if side < 2 else (ssy, rsy)
        return pltpu.make_async_remote_copy(
            src_ref=out.at[r, side % 2],
            dst_ref=land.at[r, side % 2],
            send_sem=s_sem.at[r, side % 2],
            recv_sem=r_sem.at[r, side % 2],
            device_id=sides[side][1],
            device_id_type=MESH,
        )

    def y_block(src, e, high):
        return src[pl.ds((12 if high else 0) + e, 40, stride=16), :]

    def face(src, side):
        start = 48 if side else 0
        return src[...].reshape(10, 64, LANES)[:, start : start + 16].reshape(FACE, LANES)

    def send_x(r, side, src, when=None):
        @pl.when(x_sends[r][side] if when is None else when)
        def _():
            sx[r, side] = face(src, side)
            copy_to(r, side).start()

    def send_y(r, src):
        for high in range(2):
            packed = jnp.zeros((40, LANES), f32)
            for e in range(4):
                shift = (32 * e - (96 if high else 0)) % LANES
                block = y_block(src, e, high)
                if shift:
                    block = pltpu.roll(block, shift, 1)
                packed = jnp.where(quarter == e, block, packed)

            @pl.when(y_sends[r][high])
            def _():
                sy[r, high] = packed
                copy_to(r, 2 + high).start()

    def to_operand(row, value):
        high, low = split(value)
        rows = pl.ds(row, value.shape[0])
        xb[rows, 0:LANES] = high
        xb[rows, LANES:] = low

    def products(ranges, done):
        for block in range(5):
            rows = slice(block * 128, block * 128 + 128)
            both = None
            for lo, hi in ranges:
                wide = mm(wh[rows, lo:hi], xb[lo:hi, :])
                term = wide[:, :LANES] + wide[:, LANES:] + mm(wl[rows, lo:hi], xb[lo:hi, :LANES])
                both = term if both is None else both + term
            done(rows, both)

    def begin(rows, value):
        acc[rows, :] = value

    def add(rows, value):
        acc[rows, :] = acc[rows, :] + value

    def far_value(rows, value):
        st[rows, :] = st[rows, :] + 0.5 * h * value

    def ghost_value(rows, value):
        gst[rows, :] = 0.5 * h * value

    X_ROWS = [(NODES, NODES + 2 * FACE)]
    OWN_ROWS = [(0, NODES), (NODES + 4 * FACE, KDIM)]
    FACE_ROWS = [(NODES, NODES + 4 * FACE)]

    def face_products(side, ranges):
        start = 48 if side else 0
        rows = [slice(64 * f + start, 64 * f + start + 16) for f in range(10)]
        total = None
        for lo, hi in ranges:
            left_high = jnp.concatenate([wh[r, lo:hi] for r in rows], axis=0)
            left_low = jnp.concatenate([wl[r, lo:hi] for r in rows], axis=0)
            wide = mm(left_high, xb[lo:hi, :])
            value = wide[:, :LANES] + wide[:, LANES:] + mm(left_low, xb[lo:hi, :LANES])
            total = value if total is None else total + value
        return total

    def set_x(side, value):
        to_operand(NODES + side * FACE, value)

    def span_jumps(src):
        low = src[pl.ds(0, FACE, stride=4), :]
        high = src[pl.ds(3, FACE, stride=4), :]
        near = jnp.where(span == 0, pltpu.roll(high, LANES - 24, 1), pltpu.roll(high, 8, 1))
        to_operand(NODES + 4 * FACE, near - low)
        near = jnp.where(span == 3, pltpu.roll(low, 24, 1), pltpu.roll(low, LANES - 8, 1))
        to_operand(NODES + 5 * FACE, near - high)

    def y_jumps(src, r):
        for side in (2, 3):
            @pl.when(y_sends[r][side - 2])
            def _():
                arrival(r, side).wait_recv()
        for e in range(4):
            rows = slice(40 * e, 40 * e + 40)
            low, high = y_block(src, e, 0), y_block(src, e, 1)
            far = ry[r, 0]
            if e:
                far = pltpu.roll(far, LANES - 32 * e, 1)
            jump[rows, :] = jnp.where(quarter == 0, far, pltpu.roll(high, 32, 1)) - low
            far = ry[r, 1]
            if e < 3:
                far = pltpu.roll(far, 96 - 32 * e, 1)
            rows = slice(FACE + 40 * e, FACE + 40 * e + 40)
            jump[rows, :] = jnp.where(quarter == 3, far, pltpu.roll(low, LANES - 32, 1)) - high
        to_operand(NODES + 2 * FACE, jump[...])

    def operate_own(src):
        to_operand(0, scale_lane * src[...])
        span_jumps(src)
        products(OWN_ROWS, begin)

    def operate_rest(src):
        products(FACE_ROWS, add)
        acc[...] = acc[...] - dt[...] * src[...]

    loads[3].wait()
    scale_lane = jnp.zeros((1, LANES), f32)
    for s in range(16):
        scale_lane = jnp.where(slot_of == s, scale[s], scale_lane)

    def turn(source, column):
        high, low = split(source.T)
        wh[:, column : column + source.shape[0]] = high
        wl[:, column : column + source.shape[0]] = low

    loads[4].wait()
    for block in range(5):
        turn(vol[block * 128 : block * 128 + 128, :], block * 128)
    loads[5].wait()
    for b in range(5):
        columns = slice(b * 128, b * 128 + 128)
        lfy[b] = lft[2 * FACE : 4 * FACE, columns]
        for high in range(2):
            for e in range(4):
                row = 2 * FACE + high * FACE + 40 * e
                lft[row : row + 40, columns] = lfy[b, pl.ds(high * FACE + e, 40, stride=4), :]
    for block in range(7):
        turn(lft[block * 128 : block * 128 + 128, :], NODES + block * 128)
    turn(lft[896:960, :], NODES + 896)

    loads[6].wait()
    spread16 = jnp.where(iota((16, LANES), 0) == slot_of, 1.0, 0.0).astype(bf16)
    rest = dmp[...]
    total = jnp.zeros((NODES, LANES), f32)
    for _ in range(3):
        piece = rest.astype(bf16)
        rest = rest - piece.astype(f32)
        total = total + lax.dot_general(
            piece, spread16, (((0,), (0,)), ((), ())), preferred_element_type=f32
        )
    dt[...] = total

    loads[7].wait()
    loads[8].wait()
    f00, f01, f10, f11 = part(0, 0), part(0, 1), part(1, 0), part(1, 1)

    def forcing_at(moment):
        a, b = omegas[0] * moment, omegas[1] * moment
        return (
            f00 * math.cos(a) - f01 * math.sin(a) + f10 * math.cos(b) - f11 * math.sin(b)
        )

    f1[...] = forcing_at(h)
    f2[...] = forcing_at(2 * h)

    operate_own(st)
    pl.semaphore_wait(barrier, expected)
    for side in range(2):
        send_x(0, side, st, near_side[side])
    send_y(0, st)
    for side in range(2):
        send_x(0, side, st, far_side[side])
    y_jumps(st, 0)
    for side in range(2):
        @pl.when(near_side[side])
        def _():
            arrival(0, side).wait_recv()

        @pl.when(far_side[side])
        def _():
            set_x(side, -face(st, side))

        @pl.when(jnp.logical_not(far_side[side]))
        def _():
            set_x(side, rx[0, side] - face(st, side))

    operate_rest(st)
    st[...] = 0.5 * h * (k1[...] + acc[...] + f1[...])


    def damping_copy(side):
        return pltpu.make_async_remote_copy(
            src_ref=sd, dst_ref=rd, send_sem=ssd.at[0], recv_sem=rsd.at[0],
            device_id=sides[side][1], device_id_type=MESH,
        )

    @pl.when(far_any)
    def _():
        send_y(1, st)
        for side in range(2):
            send_x(1, side, st)
        to_operand(0, scale_lane * st[...])
        span_jumps(st)
        for side in range(2):
            @pl.when(far_side[side])
            def _():
                set_x(side, -face(st, side))
                corr[1] = face_products(side, OWN_ROWS)

        y_jumps(st, 1)
        for side in range(2):
            @pl.when(far_side[side])
            def _():
                arrival(2, 1 - side).wait_recv()
                set_x(1 - side, rx[2, 1 - side] - face(st, 1 - side))
                slope = corr[1] + face_products(side, FACE_ROWS)
                slope = slope - face(dt, side) * face(st, side) + face(f1, side)
                sx[3, side] = face(st, side) + h * slope

        for side in range(2):
            @pl.when(far_side[side])
            def _():
                set_x(side, jnp.zeros((FACE, LANES), f32))
                set_x(1 - side, sx[0, side])
                mine_damped = face(dt, side)
                packed = [jnp.zeros((16, LANES), f32), jnp.zeros((16, LANES), f32)]
                for b in range(10):
                    piece = mine_damped[16 * b : 16 * b + 16]
                    packed[b // 8] = jnp.where((lane & 7) == b % 8, piece, packed[b // 8])
                sd[0:16, :] = packed[0]
                sd[16:32, :] = packed[1]
                sd[32:, :] = jnp.broadcast_to(scale_lane, (8, LANES))

        products(X_ROWS, ghost_value)
        send_y(5, gst)
        for side in range(2):
            @pl.when(far_side[side])
            def _():
                arrival(0, side).wait_recv()
                set_x(side, rx[0, side])
                set_x(1 - side, jnp.zeros((FACE, LANES), f32))
                inner = face_products(1 - side, X_ROWS)
                sx[2, 1 - side] = face(st, 1 - side) + 0.5 * h * inner
                copy_to(2, 1 - side).start()

        products(X_ROWS, far_value)

    send_y(2, st)
    for side in range(2):
        send_x(2, side, st, jnp.logical_and(near_side[side], jnp.logical_not(far_any)))
    for side in range(2):
        @pl.when(far_side[side])
        def _():
            copy_to(3, side).start()
            damping_copy(side).start()

    q1[...] = st[...]

    def keep_state(n, value):
        lanes = slice(n * LANES, n * LANES + LANES)
        high, low = split(value)
        qh[:, lanes] = high
        ql[:, lanes] = low
        high, low = split(value.T)
        th[lanes, :] = high
        tl[lanes, :] = low

    @pl.when(far_any)
    def _():
        to_operand(0, gst[...])
        span_jumps(gst)
        y_jumps(gst, 5)
        for side in range(2):
            set_x(side, -face(gst, side))
        for side in range(2):
            @pl.when(far_side[side])
            def _():
                other = 1 - side
                corr[0] = face(gst, other)
                corr[1] = face_products(other, [(0, NODES)])
                corr[2] = face_products(other, [(NODES, KDIM)])

    operate_own(st)
    y_jumps(st, 2)
    for side in range(2):
        @pl.when(jnp.logical_and(near_side[side], jnp.logical_not(far_any)))
        def _():
            arrival(2, side).wait_recv()

        @pl.when(far_side[side])
        def _():
            arrival(1, side).wait_recv()
            set_x(side, rx[1, side] + corr[0] - face(st, side))

        @pl.when(jnp.logical_not(far_side[side]))
        def _():
            set_x(side, rx[2, side] - face(st, side))

    for side in range(2):
        @pl.when(near_side[side])
        def _():
            slope = face(acc, side) + face_products(side, FACE_ROWS)
            slope = slope - face(dt, side) * face(st, side) + face(f1, side)
            sx[4, side] = face(q1, side) + h * slope
            copy_to(4, side).start()

    operate_rest(st)
    k1[...] = acc[...] + f1[...]
    st[...] = q1[...] + h * k1[...]
    send_y(4, st)
    operate_own(st)
    keep_state(0, q1[...])

    def state_products(rows, n):
        lanes = slice(n * LANES, n * LANES + LANES)
        right = jnp.concatenate([qh[:, lanes], ql[:, lanes]], axis=1)
        wide = mm(th[0:rows, :], right) + mm(tl[0:rows, :], right)
        return wide[:, :LANES] + wide[:, LANES:]

    own_pairs = state_products(LANES, 0)

    for side in range(2):
        @pl.when(far_side[side])
        def _():
            other = 1 - side
            set_x(side, jnp.zeros((FACE, LANES), f32))
            set_x(other, face(q1, side))
            direct = face_products(other, X_ROWS)
            damping_copy(side).wait_recv()
            damped = []
            for b in range(10):
                piece = rd[16 * (b // 8) : 16 * (b // 8) + 16, :]
                piece = jnp.where((lane & 7) == b % 8, piece, 0.0)
                if b % 8:
                    piece = pltpu.roll(piece, LANES - b % 8, 1)
                for shift in (1, 2, 4):
                    piece = piece + pltpu.roll(piece, shift, 1)
                damped.append(piece)
            damped = jnp.concatenate(damped, axis=0)
            change = rd[32:33, :] * corr[1] + corr[2] - damped * corr[0] + direct
            corr[0] = corr[0] + h * change

    y_jumps(st, 4)
    for side in range(2):
        @pl.when(near_side[side])
        def _():
            arrival(4, side).wait_recv()

        @pl.when(far_side[side])
        def _():
            arrival(3, side).wait_recv()
            set_x(side, rx[3, side] + corr[0] - face(st, side))

        @pl.when(jnp.logical_not(far_side[side]))
        def _():
            set_x(side, rx[4, side] - face(st, side))

    operate_rest(st)
    keep_state(1, q1[...] + 0.5 * h * (k1[...] + acc[...] + f2[...]))
    results = [
        pltpu.make_async_copy(th, qh_out, out_sem.at[0]),
        pltpu.make_async_copy(tl, ql_out, out_sem.at[1]),
    ]
    for result in results:
        result.start()

    second = state_products(2 * LANES, 1)
    cross = second[:LANES]
    pairs = jnp.concatenate(
        [
            jnp.concatenate([own_pairs, cross], axis=1),
            jnp.concatenate([cross.T, second[LANES:]], axis=1),
        ],
        axis=0,
    )
    row = iota((2 * LANES, 2 * LANES), 0)
    col = iota((2 * LANES, 2 * LANES), 1)
    pairs = jnp.where(((row >> 3) & 15) == ((col >> 3) & 15), pairs, 0.0)
    sums = jnp.sum(pairs.reshape(2, 16, 8, 2 * LANES), axis=1)
    halves = []
    for half in range(2):
        value = sums[:, :, half * LANES : half * LANES + LANES].reshape(16, LANES)
        for shift in (64, 32, 16, 8):
            value = value + pltpu.roll(value, shift, 1)
        halves.append(value)
    both = jnp.where((lane & 8) == 0, halves[0], halves[1])
    sub = iota((8, LANES), 0)
    wide = iota((8, LANES), 1)
    for t in range(2):
        picked = jnp.where((wide >> 4) == sub, both[8 * t : 8 * t + 8], 0.0)
        zs[0, t : t + 1, :] = jnp.sum(picked, axis=0, keepdims=True)

    for phase in range(2):
        copies = []
        for k in range(1, GROUP):
            copy = pltpu.make_async_remote_copy(
                src_ref=zs.at[phase],
                dst_ref=zr.at[phase, mine[phase]],
                send_sem=ssz.at[phase, k],
                recv_sem=rsz.at[phase, mine[phase]],
                device_id=partner(phase, k),
                device_id_type=MESH,
            )
            copy.start()
            copies.append(copy)
        zr[phase, mine[phase]] = zs[phase]
        for k in range(1, GROUP):
            source = (mine[phase] + k) % GROUP
            pltpu.make_async_remote_copy(
                src_ref=zs.at[phase],
                dst_ref=zr.at[phase, source],
                send_sem=ssz.at[phase, k],
                recv_sem=rsz.at[phase, source],
                device_id=partner(phase, k),
                device_id_type=MESH,
            ).wait_recv()
        total = zr[phase, 0]
        for s in range(1, GROUP):
            total = total + zr[phase, s]
        if phase == 0:
            zs[1] = total
        else:
            gram_out[...] = total
        for copy in copies:
            copy.wait_send()

    for r, sent in enumerate(x_sends):
        for side in range(2):
            @pl.when(sent[side])
            def _():
                copy_to(r, side).wait_send()
    for r, sent in enumerate(y_sends):
        for side in range(2 if sent else 0):
            @pl.when(sent[side])
            def _():
                copy_to(r, 2 + side).wait_send()
    for side in range(2):
        @pl.when(far_side[side])
        def _():
            damping_copy(side).wait_send()

    for result in results:
        result.wait()


def finish_kernel(
    unknowns, qh_hbm, ql_hbm, gram, slots_hbm, basis_out, factor_out,
    slots, qh, ql, stage, factor, load_sem, sems, factor_sem,
):
    loads = [
        pltpu.make_async_copy(slots_hbm, slots, load_sem.at[0]),
        pltpu.make_async_copy(qh_hbm, qh, load_sem.at[1]),
        pltpu.make_async_copy(ql_hbm, ql, load_sem.at[2]),
    ]
    for load in loads:
        load.start()
    sub = iota((8, LANES), 0)
    lane = iota((8, LANES), 1)
    tiles = []
    for t in range(2):
        value = jnp.where((lane >> 4) == sub, gram[t : t + 1, :], 0.0)
        for shift in (64, 32, 16):
            value = value + pltpu.roll(value, shift, 1)
        tiles.append(value)
    low = (lane & 8) == 0
    a11 = jnp.where(low, tiles[0], pltpu.roll(tiles[0], 8, 1))
    a12 = jnp.where(low, pltpu.roll(tiles[0], LANES - 8, 1), tiles[0])
    a21 = jnp.where(low, tiles[1], pltpu.roll(tiles[1], 8, 1))
    a22 = jnp.where(low, pltpu.roll(tiles[1], LANES - 8, 1), tiles[1])
    root = math.sqrt(unknowns)
    h = step_size
    work = []
    for w in range(2):
        angle = omegas[w] * h
        work.append([
            a11 + a22 + math.cos(angle) * (a12 + a21),
            math.sin(angle) * (a21 - a12),
            jnp.where((lane & 7) == sub, 1.0, 0.0),
            jnp.zeros((8, LANES), f32),
        ])
    for i in range(8):
        below, here = sub > i, sub == i
        for w in range(2):
            g_re, g_im, m_re, m_im = work[w]
            c_re = jnp.sum(jnp.where(lane == i, g_re, 0.0), axis=1, keepdims=True)
            c_im = jnp.sum(jnp.where(lane == i, g_im, 0.0), axis=1, keepdims=True)
            pivot = c_re[i : i + 1, :]
            inverse = 1.0 / jnp.sqrt(pivot)
            c_re = c_re / pivot
            c_im = c_im / pivot

            def update(re, im):
                r_re, r_im = re[i : i + 1, :], im[i : i + 1, :]
                new_re = re - (c_re * r_re - c_im * r_im)
                new_im = im - (c_re * r_im + c_im * r_re)
                return (
                    jnp.where(below, new_re, jnp.where(here, re * inverse, re)),
                    jnp.where(below, new_im, jnp.where(here, im * inverse, im)),
                )

            g_re, g_im = update(g_re, g_im)
            m_re, m_im = update(m_re, m_im)
            work[w] = [g_re, g_im, m_re, m_im]
    for w in range(2):
        g_re, g_im = work[w][:2]
        factor[w, 0] = jnp.where(lane >= sub, g_re * (h / root), 0.0)[:, :8]
        factor[w, 1] = jnp.where(lane > sub, g_im * (h / root), 0.0)[:, :8]
    copies = [pltpu.make_async_copy(factor, factor_out, factor_sem)]
    copies[0].start()
    for load in loads:
        load.wait()
    keep = (iota((LANES, LANES), 0) & 15) == lane_slots(slots)
    q_high, q_low = qh[...], ql[...]
    for w in range(2):
        m_re, m_im = work[w][2:]
        for p in range(2):
            blocks = []
            for n in range(2):
                c, s = math.cos(omegas[w] * h * (n + 1)), math.sin(omegas[w] * h * (n + 1))
                if p == 0:
                    coef = root * (c * m_re - s * m_im)
                else:
                    coef = -root * (s * m_re + c * m_im)
                coef = jnp.broadcast_to(coef[:, None, :], (8, 16, LANES)).reshape(LANES, LANES)
                blocks.append(jnp.where(keep, coef, 0.0))
            high, low_part = split(jnp.concatenate(blocks, axis=1))
            result = mm(high, q_high) + (mm(high, q_low) + mm(low_part, q_high))
            stage[w, p] = result.reshape(8, 16, NODES)
            copy = pltpu.make_async_copy(stage.at[w, p], basis_out.at[w, p], sems.at[w, p])
            copy.start()
            copies.append(copy)
    for copy in copies:
        copy.wait()


def on_device(forcing, scale, damping, volume, lift, slots):
    hbm = pl.BlockSpec(memory_space=pltpu.HBM)
    vmem = pl.BlockSpec(memory_space=pltpu.VMEM)
    state = pltpu.VMEM((NODES, LANES), f32)
    q_high, q_low, gram = pl.pallas_call(
        march_kernel,
        out_shape=(
            jax.ShapeDtypeStruct((2 * LANES, NODES), bf16),
            jax.ShapeDtypeStruct((2 * LANES, NODES), bf16),
            jax.ShapeDtypeStruct((2, LANES), f32),
        ),
        in_specs=[hbm] * 6,
        out_specs=(hbm, hbm, vmem),
        scratch_shapes=[
            pltpu.SMEM(slots.shape, jnp.int32),
            pltpu.SMEM(scale.shape, f32),
            pltpu.VMEM(forcing.shape, bf16),
            pltpu.VMEM((NODES, NODES), f32),
            pltpu.VMEM((6 * FACE, NODES), f32),
            pltpu.VMEM((5, 2 * FACE, LANES), f32),
            pltpu.VMEM((16, NODES), f32),
            pltpu.VMEM((NODES, KDIM), bf16),
            pltpu.VMEM((NODES, KDIM), bf16),
            state, state, state, state, state, state,
            pltpu.VMEM((2 * FACE, LANES), f32),
            pltpu.VMEM((KDIM, 2 * LANES), bf16),
            state,
            pltpu.VMEM((NODES, 2 * LANES), bf16),
            pltpu.VMEM((NODES, 2 * LANES), bf16),
            pltpu.VMEM((2 * LANES, NODES), bf16),
            pltpu.VMEM((2 * LANES, NODES), bf16),
            pltpu.VMEM((3, FACE, LANES), f32),
            state,
            pltpu.VMEM((40, LANES), f32),
            pltpu.VMEM((40, LANES), f32),
            pltpu.VMEM((5, 2, FACE, LANES), f32),
            pltpu.VMEM((6, 2, 40, LANES), f32),
            pltpu.VMEM((5, 2, FACE, LANES), f32),
            pltpu.VMEM((6, 2, 40, LANES), f32),
            pltpu.VMEM((2, 2, LANES), f32),
            pltpu.VMEM((2, GROUP, 2, LANES), f32),
            pltpu.SemaphoreType.DMA((9,)),
            pltpu.SemaphoreType.DMA((5, 2)),
            pltpu.SemaphoreType.DMA((5, 2)),
            pltpu.SemaphoreType.DMA((6, 2)),
            pltpu.SemaphoreType.DMA((6, 2)),
            pltpu.SemaphoreType.DMA((1,)),
            pltpu.SemaphoreType.DMA((1,)),
            pltpu.SemaphoreType.DMA((2, GROUP)),
            pltpu.SemaphoreType.DMA((2, GROUP)),
            pltpu.SemaphoreType.DMA((2,)),
        ],
        compiler_params=pltpu.CompilerParams(
            collective_id=0, has_side_effects=True, vmem_limit_bytes=64 * 1024 * 1024
        ),
        name="march",
    )(forcing, scale, damping, volume, lift, slots)
    unknowns = forcing.shape[3] * NODES * lax.axis_size("gx") * lax.axis_size("gy")
    shape = forcing.shape
    return pl.pallas_call(
        lambda *refs: finish_kernel(unknowns, *refs),
        out_shape=(
            jax.ShapeDtypeStruct(shape, f32),
            jax.ShapeDtypeStruct((2, 2, 8, 8), f32),
        ),
        in_specs=[hbm, hbm, vmem, hbm],
        out_specs=(hbm, hbm),
        scratch_shapes=[
            pltpu.SMEM(slots.shape, jnp.int32),
            pltpu.VMEM((2 * LANES, NODES), bf16),
            pltpu.VMEM((2 * LANES, NODES), bf16),
            pltpu.VMEM(shape, f32),
            pltpu.VMEM((2, 2, 8, 8), f32),
            pltpu.SemaphoreType.DMA((3,)),
            pltpu.SemaphoreType.DMA((2, 2)),
            pltpu.SemaphoreType.DMA,
        ],
        compiler_params=pltpu.CompilerParams(vmem_limit_bytes=64 * 1024 * 1024),
        name="finish",
    )(q_high, q_low, gram, slots)


def solution(mesh):
    placed = (
        P(None, None, None, ("gx", "gy"), None),
        P(("gx", "gy")),
        P(("gx", "gy"), None),
        P(),
        P(),
        P("gx", "gy", None),
    )
    return jax.shard_map(
        on_device,
        mesh=mesh,
        in_specs=placed,
        out_specs=(P(None, None, None, ("gx", "gy"), None), P()),
        check_vma=False,
    )
```
